32 devices in a mesh: det: 4 (over x, core), pix: 8 (over z, y).
Axes of the slice: x: 2, y: 2, z: 4, core: 2. Of those that a mesh axis runs over, the one named last changes fastest.
Arguments:
- timestream: float32 [32, 256, 128], P(('det', 'pix')), may hold values from -48 to 48
- weights: bfloat16 [32, 256, 128, 256], P(('det', 'pix')), may hold values from 0.0004 to 1
- block_owner: int32 [32, 256, 1], P(('det', 'pix')), may hold values from 0 to 7; in each aligned block of 256 rows (0 to 255, 256 to 511, ..., all dimensions but the last counted through in order) at most 64 rows name the same one
- block_local: int32 [32, 256], P(('det', 'pix')), may hold values from 0 to 63
- baseline_of: int32 [32, 256], P(('det', 'pix')), may hold values from 0 to 127, never falling along the last dimension, each value on 1 to 3 neighbouring positions
Outputs:
- offset_levels: float32 [32, 128], P(('det', 'pix'))
- leftover_error: float32 [32, 128], P(('det', 'pix'))
The draws below stay inside these ranges and needn't reach their ends.
Inputs may be any that keep to these rules, and one draw needn't show every extreme that they name: `block_owner`: among the 256 blocks of one timestream row at most 64 name the same owner, and in every row some owner is named by exactly 64. `baseline_of`: along each row the baseline index never falls; each of the 128 baselines covers 1 to 3 blocks, and some covers exactly 3.
All inputs are finite; a program needn't handle non-finite values.
Results may differ from the reference program's by a relative error of at most 0.013.
Values may be sent and summed in bfloat16 or wider, within the bound.
No kernel may reach another device: no remote copies, remote signals or barrier semaphores. Data moves between devices by JAX's collectives and lax.ppermute only.
A program may use at most 64 MiB of HBM per device.

```python
import math
import jax
import jax.numpy as jnp
import numpy as np
from jax import lax

SAMP = 128
PIX = 256
NBLK_DEV = 256
PB_DEV = 64
ITERS = 2
CAP = 64
NBASE_DEV = 128
N_TOD = 32
NPB = 512
N_PIX = 8


def pointing_common(key):
    keys = jax.random.split(jax.random.fold_in(key, 7), 3)
    shape = (N_TOD, NBLK_DEV, SAMP)
    candidates = jax.random.randint(keys[0], (3,) + shape, 0, PIX - 1)
    pointed = jnp.min(candidates, axis=0).astype(jnp.int32)
    fraction = jax.random.uniform(keys[1], shape, jnp.float32, 0.05, 1.0)
    pattern = jax.random.uniform(keys[2], (PIX,), jnp.float32, -1.0, 1.0)
    return (pointed, fraction, pattern)


def draw_weights(key, part):
    pointed, fraction, pattern = pointing_common(key)
    floor_key = jax.random.fold_in(key, 11)
    shape = (N_TOD, NBLK_DEV, SAMP, PIX)
    floor_vals = jnp.exp(jax.random.uniform(floor_key, shape, jnp.float32, jnp.log(0.0005), jnp.log(0.005)))
    column = jnp.arange(PIX, dtype=jnp.int32)
    first_col = pointed[..., None]
    values = jnp.where(column == first_col, 1.0, jnp.where(column == first_col + 1, fraction[..., None], floor_vals))
    return values.astype(jnp.float32).astype(jnp.bfloat16)


def draw_timestream(key, part):
    pointed, fraction, pattern = pointing_common(key)
    keys = jax.random.split(jax.random.fold_in(key, 13), 2)
    shape = (N_TOD, NBLK_DEV, SAMP)
    sky_values = pattern
    noise = 4.0 * jax.random.normal(keys[0], shape, jnp.float32)
    offsets = 3.0 * jax.random.normal(keys[1], (N_TOD, NBLK_DEV, 1), jnp.float32)
    signal = 30.0 * (jnp.take(sky_values, pointed) + fraction * jnp.take(sky_values, pointed + 1)) / (1.0 + fraction)
    return jnp.clip(signal + offsets + noise, -48.0, 48.0).astype(jnp.float32)


def touch_ends(entries, stream_key, low, high):
    longest = entries.shape.index(max(entries.shape))
    spots = []
    for shift in (0, 1):
        where = [jax.random.randint(jax.random.fold_in(stream_key, axis), (), 0, length) for axis, length in enumerate(entries.shape)]
        where[longest] = (where[longest] + shift) % entries.shape[longest]
        spots.append(tuple(where))
    return entries.at[spots[0]].set(low).at[spots[1]].set(high)


def length_profile(count, total, most, lean):
    weights = [(1 << 20) // math.isqrt(grade ** lean) + 1 for grade in range(2, count + 1)]
    spare, holding = total - most - (count - 1), [1] * (count - 1)
    while spare > 0:
        movable = [i for i in range(count - 1) if holding[i] < most]
        mass, left = sum([weights[i] for i in movable]), spare
        for i in movable:
            more = min(most - holding[i], max(1, left * weights[i] // mass), spare)
            holding[i] = holding[i] + more
            spare = spare - more
    return np.array([most] + holding)


def ragged(stream_key, number_of, total, bound, lean):
    if number_of == 2:
        one = jax.random.randint(stream_key, (), max(1, total - bound), min(bound, total - 1) + 1)
        return jnp.stack([one, total - one])
    tallies = jnp.asarray(length_profile(number_of, total, bound, lean), jnp.int32)
    pairs = (number_of - 1) // 2
    donor, sink = tallies[1:1 + 2 * pairs:2], tallies[2:2 + 2 * pairs:2]
    room = jnp.minimum(donor - 1, bound - sink)
    shifted = jax.random.randint(jax.random.fold_in(stream_key, 1), (pairs,), 0, 1 << 20) % (room + 1)
    tallies = tallies.at[1:1 + 2 * pairs:2].set(donor - shifted).at[2:2 + 2 * pairs:2].set(sink + shifted)
    return tallies[jax.random.permutation(jax.random.fold_in(stream_key, 2), number_of)]


def assign_block(stream_key, own, number, rows, count, top, bound, skew):
    sequence = jax.random.permutation(stream_key, count)
    crowded, ordinary = shares(count, rows * top, bound, skew, True), shares(count, rows * top, bound, skew, False)
    places = jnp.arange(count)

    def named(lengths, offset_by):
        used = int((lengths > 0).sum())
        fixed = max(1, used // 4)
        shifted = fixed + (places - fixed + offset_by * (used - fixed)) % max(1, count - fixed)
        return jnp.zeros((count,), jnp.int32).at[sequence[jnp.where(places < fixed, places, shifted)]].set(jnp.asarray(lengths, jnp.int32))

    lengths = jnp.where(number % 4 == 0, named(crowded, number // 4), named(ordinary, number - number // 4 - 1))
    mixed = jax.random.permutation(jax.random.fold_in(own, 3), count)
    donor, receiver = mixed[0:count // 2 * 2:2], mixed[1:count // 2 * 2:2]
    room = jnp.minimum(lengths[donor] - 1, bound - lengths[receiver]) // 2
    room = jnp.where((donor == sequence[0]) | (receiver == sequence[0]) | (lengths[receiver] == 0), 0, jnp.maximum(room, 0))
    shifted = jax.random.randint(jax.random.fold_in(own, 4), (count // 2,), 0, 1 << 20) % (room + 1)
    lengths = lengths.at[donor].add(-shifted).at[receiver].add(shifted)
    items = jnp.searchsorted(jnp.cumsum(lengths), jnp.arange(rows * top), side="right").astype(jnp.int32)
    grid = items.reshape(top, rows).T
    grid = grid[jax.random.permutation(jax.random.fold_in(own, 1), rows)]
    offset_by = jax.random.randint(jax.random.fold_in(own, 2), (rows, 1), 0, top)
    return jnp.take_along_axis(grid, (jnp.arange(top)[None, :] + offset_by) % top, axis=1)


def shares(count, total, reach, lean, full):
    loads = [(1 << 20) // math.isqrt(rank ** lean) + 1 for rank in range(1, count + 1)]
    largest = reach if full else min(reach, max(-(-total // count), total * loads[0] // sum(loads)))
    least = 1 if total - largest >= count - 1 else 0
    counts, rest = [largest] + [least] * (count - 1), total - largest - least * (count - 1)
    while rest > 0:
        free = [i for i in range(1, count) if counts[i] < largest] or [i for i in range(1, count) if counts[i] < reach]
        pool, left = sum([loads[i] for i in free]), rest
        for i in free:
            extra = min(reach - counts[i], max(1, left * loads[i] // pool), rest)
            counts[i] = counts[i] + extra
            rest = rest - extra
    return np.array(counts)


def setup_inputs(seed: int = 0) -> dict:
    splits = jax.random.split(jax.random.key(seed), 6)
    timestream = draw_timestream(jax.random.fold_in(splits[5], 71), 0)
    weights = draw_weights(jax.random.fold_in(splits[5], 71), 0)
    block_owner_keys = jax.random.split(jax.random.fold_in(splits[2], 1), N_TOD * NBLK_DEV // NBLK_DEV)
    block_owner_turns = jax.random.permutation(jax.random.fold_in(splits[2], 3), N_TOD * NBLK_DEV // NBLK_DEV)
    block_owner = jax.vmap(lambda own, number: assign_block(jax.random.fold_in(splits[2], 2), own, number, NBLK_DEV, N_PIX, 1, CAP, 2))(block_owner_keys, block_owner_turns).reshape((N_TOD, NBLK_DEV, 1))
    block_local = touch_ends(jax.random.randint(splits[3], (N_TOD, NBLK_DEV), 0, PB_DEV), jax.random.fold_in(splits[3], 1), 0, PB_DEV - 1).astype(jnp.int32)
    baseline_of = jax.vmap(lambda own: jnp.searchsorted(jnp.cumsum(ragged(own, NBASE_DEV, NBLK_DEV, 3, 0)), jnp.arange(NBLK_DEV), side="right"))(jax.random.split(splits[4], N_TOD)).reshape((N_TOD, NBLK_DEV)).astype(jnp.int32)
    return {"timestream": timestream, "weights": weights, "block_owner": block_owner, "block_local": block_local, "baseline_of": baseline_of}


def reference(timestream, weights, block_owner, block_local, baseline_of):
    block_pix = (block_owner[:, :, 0] * PB_DEV + block_local).astype(jnp.int32)
    flat_pix = block_pix.reshape(-1)

    def bin_terms(series_b):
        def one_row(pair):
            weight_row, series_row = pair
            return jnp.einsum('kbs,bsp->kbp', series_row.astype(jnp.float32), weight_row.astype(jnp.float32))
        terms = lax.map(one_row, (weights, jnp.swapaxes(series_b, 0, 1)))
        count_k = series_b.shape[0]
        terms = jnp.swapaxes(terms, 0, 1).reshape(count_k, -1, PIX)
        return jax.vmap(lambda values: jax.ops.segment_sum(values, flat_pix, num_segments=NPB))(terms)

    def project_map(map_b):
        def one_row(pair):
            weight_row, pix_row = pair
            return jnp.einsum('bsp,bp->bs', weight_row.astype(jnp.float32), map_b[pix_row].astype(jnp.float32))
        return lax.map(one_row, (weights, block_pix))

    def collapse(series):
        per_block = jnp.sum(series, axis=-1)
        return jax.vmap(lambda values, segs: jax.ops.segment_sum(values, segs, num_segments=NBASE_DEV))(per_block, baseline_of)

    def expand(amps):
        per_block = jnp.take_along_axis(amps, baseline_of, axis=1)
        return jnp.broadcast_to(per_block[:, :, None], (per_block.shape[0], per_block.shape[1], SAMP))

    row_sums = lax.map(lambda weight_row: jnp.sum(weight_row.astype(jnp.float32), axis=-1), weights).astype(jnp.bfloat16)
    first = bin_terms(jnp.stack([row_sums, timestream.astype(jnp.bfloat16)]))
    hit_sums = first[0]
    sky_map = first[1] / (hit_sums + 1.0)
    projected = project_map(sky_map.astype(jnp.bfloat16))
    equation_target = collapse(timestream - projected) / SAMP

    def normal_equations_action(amps):
        series = expand(amps)
        binned = bin_terms(series.astype(jnp.bfloat16)[None])[0]
        sky = binned / (hit_sums + 1.0)
        proj = project_map(sky.astype(jnp.bfloat16))
        return collapse(series - proj) / SAMP + amps

    offset_levels = jnp.zeros_like(equation_target)
    leftover_error = equation_target
    descent_heading = equation_target
    current_norm = jnp.sum(leftover_error * leftover_error)
    for iteration in range(ITERS):
        image = normal_equations_action(descent_heading)
        descent_factor = current_norm / jnp.sum(descent_heading * image)
        offset_levels = offset_levels + descent_factor * descent_heading
        leftover_error = leftover_error - descent_factor * image
        norm_next = jnp.sum(leftover_error * leftover_error)
        descent_heading = leftover_error + (norm_next / current_norm) * descent_heading
        current_norm = norm_next
    return offset_levels, leftover_error
```

```python
import functools

import jax
import jax.numpy as jnp
from jax import lax
from jax.experimental import pallas as pl
from jax.experimental.pallas import tpu as pltpu
from jax.sharding import PartitionSpec as P

PB_DEV = 64
NBASE_DEV = 128
CAP = 64
LANES = 128
AXES = ("det", "pix")
BF = jnp.bfloat16
F32 = jnp.float32
VMEM_LIMIT = 48 * 1024 * 1024


def dot_nn(a, b):
    return lax.dot_general(a, b, (((1,), (0,)), ((), ())), preferred_element_type=F32)


def dot_nt(a, b):
    return lax.dot_general(a, b, (((1,), (1,)), ((), ())), preferred_element_type=F32)


def split3(v):
    a = v.astype(BF)
    left = v - a.astype(F32)
    b = left.astype(BF)
    c = (left - b.astype(F32)).astype(BF)
    return a, b, c


def iota(shape, dim):
    return lax.broadcasted_iota(jnp.int32, shape, dim)


def bin_kernel(n_det, n_pix, group, ts_ref, w_ref, own_ref, loc_ref, base_ref, out_ref, col_s, hit_s, dat_s):
    step = pl.program_id(0)
    blocks, samples = ts_ref.shape[1], ts_ref.shape[2]
    pixels = w_ref.shape[3]
    row = iota((8, samples), 0)
    ones = jnp.ones((8, pixels), BF)
    lhs = []
    for j in range(group):
        r = dot_nt(ones, w_ref[0, j])
        u = jnp.broadcast_to(ts_ref[0, pl.ds(step * group + j, 1), :], (8, samples))
        lhs.append(jnp.where(row == 0, r, jnp.where(row == 1, u, 1.0)).astype(BF))
    for j in range(group):
        t = dot_nn(lhs[j], w_ref[0, j])
        where = pl.ds(step * group + j, 1)
        hit_s[where, :] = t[0:1]
        dat_s[where, :] = t[1:2]
        col_s[where, :] = t[2:3]

    @pl.when(step == pl.num_programs(0) - 1)
    def _():
        pch = pixels // n_det
        half = pch // 2
        wide = n_pix * LANES
        own = own_ref[0]
        loc_row = loc_ref[...].astype(F32).astype(BF)
        base_row = base_ref[...].astype(F32).astype(BF)
        eye = (iota((blocks, blocks), 0) == iota((blocks, blocks), 1)).astype(F32).astype(BF)
        loc = dot_nt(eye, jnp.broadcast_to(loc_row, (8, blocks)))[:, 0:1].astype(jnp.int32)
        tri = (iota((blocks, blocks), 1) < iota((blocks, blocks), 0)).astype(F32).astype(BF)
        own_hot = (own == iota((blocks, LANES), 1)).astype(F32)
        before = dot_nn(tri, own_hot.astype(BF))
        pos = jnp.sum(before * own_hot, axis=1, keepdims=True).astype(jnp.int32)
        lane = iota((blocks, wide), 1)

        def hot(target):
            return (lane == target).astype(F32).astype(BF)

        slot_lo, slot_hi = hot(own * LANES + pos), hot(own * LANES + PB_DEV + pos)
        pb_lo, pb_hi = hot(own * LANES + loc), hot(own * LANES + PB_DEV + loc)
        col_t = col_s[...].T.astype(BF)
        hit_t = hit_s[...].T.astype(BF)
        dat_t = dat_s[...].T.astype(BF)
        both = (dot_nn(col_t, slot_lo) + dot_nn(hit_t, pb_hi)).astype(BF)
        first = jnp.concatenate([dat_t[d * pch : d * pch + half] for d in range(n_det)], axis=0)
        second = jnp.concatenate([dat_t[d * pch + half : (d + 1) * pch] for d in range(n_det)], axis=0)
        data = (dot_nn(first, pb_lo) + dot_nn(second, pb_hi)).astype(BF)
        where = dot_nn(jnp.broadcast_to(loc_row, (8, blocks)), slot_lo) + dot_nn(jnp.broadcast_to(base_row, (8, blocks)), slot_hi)

        base_t = iota((NBASE_DEV, blocks), 0) == base_ref[...]
        base_hot = base_t.astype(F32).astype(BF)
        t0, t1, t2 = split3(ts_ref[0])
        per_base = dot_nn(base_hot, t0) + dot_nn(base_hot, t1) + dot_nn(base_hot, t2)
        b0, b1, b2 = split3(per_base)
        one = jnp.ones((8, samples), BF)
        total = dot_nt(one, b0) + dot_nt(one, b1) + dot_nt(one, b2)
        s0, s1, s2 = split3(total)
        count = dot_nt(jnp.ones((8, blocks), BF), base_hot)
        r16 = iota((16, LANES), 0)

        def rep(v):
            v = v.astype(F32)
            return jnp.concatenate([v, v], axis=0)

        own_rows = jnp.where(r16 == 1, rep(s0), jnp.where(r16 == 2, rep(s1), jnp.where(r16 == 3, rep(s2), rep(count))))
        for o in range(n_pix):
            cols = slice(o * LANES, (o + 1) * LANES)
            tile = jnp.where(r16 == 0, rep(where[:, cols]), own_rows).astype(BF)
            for d in range(n_det):
                to = d * n_pix + o
                out_ref[to, 0:pch, :] = both[d * pch : (d + 1) * pch, cols]
                out_ref[to, pch : pch + half, :] = data[d * half : (d + 1) * half, cols]
                out_ref[to, pch + half :, :] = tile


def project(col_t, sky_t, pb_hot, base_hot, row_hot):
    spread = dot_nn(sky_t.astype(BF), pb_hot)
    per_slot = jnp.sum(col_t.astype(F32) * spread, axis=0, keepdims=True)
    parts = [jnp.where(row_hot, p.astype(F32), 0.0).astype(BF) for p in split3(per_slot)]
    return dot_nt(parts[0], base_hot) + dot_nt(parts[1], base_hot) + dot_nt(parts[2], base_hot)


def bin_amps(amps, col_t, pb_hot, base_hot, row_hot):
    a0, a1, a2 = split3(amps)
    spread = dot_nn(a0, base_hot) + dot_nn(a1, base_hot) + dot_nn(a2, base_hot)
    per_slot = jnp.sum(jnp.where(row_hot, spread, 0.0), axis=0, keepdims=True)
    terms = col_t.astype(F32) * per_slot
    high = terms.astype(BF)
    low = (terms - high.astype(F32)).astype(BF)
    return dot_nt(high, pb_hot) + dot_nt(low, pb_hot)


def hots(idx_ref):
    slots = idx_ref.shape[1]
    pb_hot = (iota((PB_DEV, slots), 0).astype(F32) == idx_ref[0:1, :]).astype(F32).astype(BF)
    base_hot = (iota((NBASE_DEV, slots), 0).astype(F32) == idx_ref[1:2, :]).astype(F32).astype(BF)
    return pb_hot, base_hot


def row_mask(rows, slots):
    return iota((rows, slots), 1) // CAP == iota((rows, slots), 0)


def owner_kernel(pch, got_ref, send_ref, col_ref, idx_ref, inv_ref, base_ref, count_ref):
    rows = got_ref.shape[0]
    half = pch // 2
    low = iota((pch, LANES), 1) < CAP
    low8 = iota((16, LANES), 1) < CAP
    hits = jnp.zeros((pch, LANES), F32)
    data = jnp.zeros((half, LANES), F32)
    for i in range(rows // 2):
        a, b = got_ref[2 * i, 0:pch, :].astype(F32), got_ref[2 * i + 1, 0:pch, :].astype(F32)
        hits = hits + a + b
        data = data + got_ref[2 * i, pch : pch + half, :].astype(F32) + got_ref[2 * i + 1, pch : pch + half, :].astype(F32)
        cols = slice(i * LANES, (i + 1) * LANES)
        col_ref[:, cols] = jnp.where(low, a, pltpu.roll(b, CAP, 1)).astype(BF)
        ta, tb = got_ref[2 * i, pch + half :, :].astype(F32), got_ref[2 * i + 1, pch + half :, :].astype(F32)
        pb = jnp.where(low8, ta, pltpu.roll(tb, CAP, 1))
        base = jnp.where(low8, pltpu.roll(ta, CAP, 1), tb)
        idx_ref[0:1, cols] = pb[0:1]
        idx_ref[1:2, cols] = base[0:1]
        for g, t in ((2 * i, ta), (2 * i + 1, tb)):
            base_ref[g : g + 1, :] = t[1:2] + t[2:3] + t[3:4]
            count_ref[g : g + 1, :] = t[4:5]
    inv = 1.0 / (hits[:, CAP:] + 1.0)
    inv_ref[...] = inv
    sky = jnp.concatenate([data[:, :PB_DEV], data[:, PB_DEV:]], axis=0) * inv
    pb_hot, base_hot = hots(idx_ref)
    part = project(col_ref[...], sky, pb_hot, base_hot, row_mask(rows, col_ref.shape[1])).astype(BF)
    for g in range(rows):
        send_ref[g] = part


def total_of(got_ref):
    acc = got_ref[0].astype(F32)
    for g in range(1, got_ref.shape[0]):
        acc = acc + got_ref[g].astype(F32)
    return acc


def first_kernel(samples, got_ref, col_ref, idx_ref, inv_ref, base_ref, send_ref, rhs_ref):
    rhs = (base_ref[...] - total_of(got_ref)) * (1.0 / samples)
    rhs_ref[...] = rhs
    pb_hot, base_hot = hots(idx_ref)
    row_hot = row_mask(rhs.shape[0], col_ref.shape[1])
    binned = bin_amps(rhs, col_ref[...], pb_hot, base_hot, row_hot)
    part = project(col_ref[...], binned * inv_ref[...], pb_hot, base_hot, row_hot).astype(BF)
    for g in range(send_ref.shape[0]):
        send_ref[g] = part


def second_kernel(samples, got_ref, col_ref, idx_ref, inv_ref, rhs_ref, count_ref, send_ref, state_ref):
    rhs = rhs_ref[...]
    more = count_ref[...] + 1.0
    image = more * rhs - total_of(got_ref) * (1.0 / samples)
    rr = jnp.sum(rhs * rhs)
    alpha = rr / jnp.sum(rhs * image)
    levels = alpha * rhs
    error = rhs - alpha * image
    new = jnp.sum(error * error)
    heading = error + (new / rr) * rhs
    curve = jnp.sum(more * heading * heading)
    pb_hot, base_hot = hots(idx_ref)
    rows = rhs.shape[0]
    row_hot = row_mask(rows, col_ref.shape[1])
    binned = bin_amps(heading, col_ref[...], pb_hot, base_hot, row_hot)
    sky = binned * inv_ref[...]
    quad = jnp.sum(binned * sky)
    part = project(col_ref[...], sky, pb_hot, base_hot, row_hot)
    for g in range(rows):
        send_ref[g, 0:1, 0:LANES] = part[g : g + 1]
        send_ref[g, 0:1, LANES:] = jnp.full((1, LANES), quad, F32)
    state_ref[0] = levels
    state_ref[1] = error
    state_ref[2] = heading
    state_ref[3] = more * heading
    state_ref[4] = jnp.full((rows, LANES), new, F32)
    state_ref[5] = jnp.full((rows, LANES), curve, F32)


def last_kernel(samples, n_pix, got_ref, state_ref, levels_ref, error_ref):
    me = lax.axis_index("det") * n_pix + lax.axis_index("pix")
    acc = got_ref[0]
    for g in range(1, got_ref.shape[0]):
        acc = acc + got_ref[g]
    acc = acc * (1.0 / samples)
    mine = [state_ref[k, pl.ds(me, 1), :] for k in range(6)]
    levels, error, heading, scaled, new, curve = mine
    image = scaled - acc[:, 0:LANES]
    alpha = new / (curve - acc[:, LANES:])
    levels_ref[...] = levels + alpha * heading
    error_ref[...] = error - alpha * image


def call(kernel, outs, *args, **kw):
    vmem = pl.BlockSpec(memory_space=pltpu.VMEM)
    return pl.pallas_call(
        kernel,
        out_shape=outs,
        in_specs=[vmem] * len(args),
        out_specs=[vmem] * len(outs),
        compiler_params=pltpu.CompilerParams(vmem_limit_bytes=VMEM_LIMIT),
        **kw,
    )(*args)


def exchange(x):
    return lax.all_to_all(x, AXES, split_axis=0, concat_axis=0, tiled=True)


def body(timestream, weights, block_owner, block_local, baseline_of):
    n_det, n_pix = lax.axis_size("det"), lax.axis_size("pix")
    rows = n_det * n_pix
    _, blocks, samples, pixels = weights.shape
    pch = pixels // n_det
    slots = rows * CAP
    group = 16
    whole = lambda *shape: pl.BlockSpec(shape, lambda i: (0,) * len(shape))
    tall = pch + pch // 2 + 16
    sent = pl.pallas_call(
        functools.partial(bin_kernel, n_det, n_pix, group),
        grid=(blocks // group,),
        out_shape=jax.ShapeDtypeStruct((rows, tall, LANES), BF),
        in_specs=[
            whole(1, blocks, samples),
            pl.BlockSpec((1, group, samples, pixels), lambda i: (0, i, 0, 0)),
            whole(1, blocks, 1),
            whole(1, blocks),
            whole(1, blocks),
        ],
        out_specs=whole(rows, tall, LANES),
        scratch_shapes=[pltpu.VMEM((blocks, pixels), F32)] * 3,
        compiler_params=pltpu.CompilerParams(vmem_limit_bytes=VMEM_LIMIT, dimension_semantics=("arbitrary",)),
    )(timestream, weights, block_owner, block_local, baseline_of)
    got = exchange(sent)
    shape = jax.ShapeDtypeStruct
    everyone = shape((rows, rows, NBASE_DEV), BF)
    vector = shape((rows, NBASE_DEV), F32)
    part, col_t, idx, inv, base, count = call(
        functools.partial(owner_kernel, pch),
        [everyone, shape((pch, slots), BF), shape((8, slots), F32), shape((pch, PB_DEV), F32), vector, vector],
        got,
    )
    part, rhs = call(
        functools.partial(first_kernel, samples), [everyone, vector], exchange(part), col_t, idx, inv, base
    )
    part, state = call(
        functools.partial(second_kernel, samples),
        [shape((rows, 1, 2 * LANES), F32), shape((6, rows, NBASE_DEV), F32)],
        exchange(part), col_t, idx, inv, rhs, count,
    )
    own = shape((1, NBASE_DEV), F32)
    return tuple(call(functools.partial(last_kernel, samples, n_pix), [own, own], exchange(part), state))


def solution(mesh):
    placed = (
        P(AXES, None, None),
        P(AXES, None, None, None),
        P(AXES, None, None),
        P(AXES, None),
        P(AXES, None),
    )
    return jax.shard_map(
        body,
        mesh=mesh,
        in_specs=placed,
        out_specs=(P(AXES, None), P(AXES, None)),
        check_vma=False,
    )
```

```python
import functools

import jax
import jax.numpy as jnp
from jax import lax
from jax.experimental import pallas as pl
from jax.experimental.pallas import tpu as pltpu
from jax.sharding import PartitionSpec as P

PB_DEV = 64
NBASE_DEV = 128
CAP = 64
LANES = 128
AXES = ("det", "pix")
BF = jnp.bfloat16
F32 = jnp.float32
VMEM_LIMIT = 48 * 1024 * 1024


def dot_nn(a, b):
    return lax.dot_general(a, b, (((1,), (0,)), ((), ())), preferred_element_type=F32)


def dot_nt(a, b):
    return lax.dot_general(a, b, (((1,), (1,)), ((), ())), preferred_element_type=F32)


def split3(v):
    a = v.astype(BF)
    left = v - a.astype(F32)
    b = left.astype(BF)
    c = (left - b.astype(F32)).astype(BF)
    return a, b, c


def iota(shape, dim):
    return lax.broadcasted_iota(jnp.int32, shape, dim)


def bin_kernel(
    n_det, n_pix, group, ts_hbm, w_hbm, own_hbm, loc_hbm, base_hbm, mine_ref, give_ref, rest_ref,
    w_s, ts_s, own_s, loc_s, base_s, col_s, hit_s, dat_s, slot_lo, slot_hi, pb_lo, pb_hi, sem, small,
):
    blocks, samples, pixels = w_s.shape
    steps = blocks // group

    def weights(c):
        where = pl.ds(c * group, group)
        return pltpu.make_async_copy(w_hbm.at[0, where], w_s.at[where], sem.at[c])

    little = [
        pltpu.make_async_copy(src, dst, small.at[k])
        for k, (src, dst) in enumerate(((ts_hbm, ts_s), (own_hbm, own_s), (loc_hbm, loc_s), (base_hbm, base_s)))
    ]
    for copy in little:
        copy.start()
    for c in range(steps):
        weights(c).start()
    for copy in little:
        copy.wait()

    wide = n_pix * LANES
    loc_row = loc_s[...].astype(F32).astype(BF)
    base_row = base_s[...].astype(F32).astype(BF)
    eye = (iota((blocks, blocks), 0) == iota((blocks, blocks), 1)).astype(F32).astype(BF)
    tri = (iota((blocks, blocks), 1) < iota((blocks, blocks), 0)).astype(F32).astype(BF)
    loc = dot_nt(eye, jnp.broadcast_to(loc_row, (8, blocks)))[:, 0:1].astype(jnp.int32)
    own_row = own_s[...].astype(F32).astype(BF)
    own = dot_nt(eye, jnp.broadcast_to(own_row, (8, blocks)))[:, 0:1].astype(jnp.int32)
    own_hot = (own == iota((blocks, LANES), 1)).astype(F32)
    before = dot_nn(tri, own_hot.astype(BF))
    pos = jnp.sum(before * own_hot, axis=1, keepdims=True).astype(jnp.int32)
    lane = iota((blocks, wide), 1)

    def hot(target):
        return (lane == target).astype(F32).astype(BF)

    slot_lo[...], slot_hi[...] = hot(own * LANES + pos), hot(own * LANES + PB_DEV + pos)
    pb_lo[...], pb_hi[...] = hot(own * LANES + loc), hot(own * LANES + PB_DEV + loc)
    row = iota((8, samples), 0)
    place = iota((samples, LANES), 1)

    def row_sums(c):
        acc = jnp.zeros((samples, LANES), F32)
        for j in range(group):
            w = w_s[c * group + j].astype(F32)
            halves = w[:, 0:LANES]
            for k in range(LANES, pixels, LANES):
                halves = halves + w[:, k : k + LANES]
            acc = jnp.where(place == j, jnp.sum(halves, axis=1, keepdims=True), acc)
        return acc.T[0:group]

    def terms(c, sums):
        for j in range(group):
            r = jnp.broadcast_to(sums[j : j + 1], (8, samples))
            u = jnp.broadcast_to(ts_s[0, pl.ds(c * group + j, 1), :], (8, samples))
            lhs = jnp.where(row == 0, r, jnp.where(row == 1, u, 1.0)).astype(BF)
            t = dot_nn(lhs, w_s[c * group + j])
            where = pl.ds(c * group + j, 1)
            hit_s[where, :] = t[0:1]
            dat_s[where, :] = t[1:2]
            col_s[where, :] = t[2:3]

    def step(c, sums):
        weights(c).wait()
        after = row_sums(c)
        terms(c - 1, sums)
        return after

    weights(0).wait()
    sums = lax.fori_loop(1, steps, step, row_sums(0))
    terms(steps - 1, sums)

    pch = pixels // n_det
    half = pch // 2
    core = lax.rem(lax.axis_index("det"), 2)
    hit_s[...] = hit_s[...].T
    dat_s[...] = dat_s[...].T

    def part(of, which):
        rows = [of[pl.ds(pl.multiple_of(d * pch + which * half, half), half), :] for d in range(n_det)]
        return jnp.concatenate(rows, axis=0).astype(BF)

    def binned(which):
        return dot_nn(part(hit_s, which), pb_lo[...]) + dot_nn(part(dat_s, which), pb_hi[...])

    theirs, mine = binned(1 - core), binned(core)
    col_t = col_s[...].T.astype(BF)
    low = jnp.concatenate([col_t[d * pch : d * pch + half] for d in range(n_det)], axis=0)
    high = jnp.concatenate([col_t[d * pch + half : (d + 1) * pch] for d in range(n_det)], axis=0)
    columns = (dot_nn(low, slot_lo[...]) + dot_nn(high, slot_hi[...])).astype(BF)
    where = dot_nn(jnp.broadcast_to(loc_row, (8, blocks)), slot_lo[...])
    where = where + dot_nn(jnp.broadcast_to(base_row, (8, blocks)), slot_hi[...])

    base_hot = (iota((NBASE_DEV, blocks), 0) == base_s[...]).astype(F32).astype(BF)
    t0, t1, t2 = split3(ts_s[0])
    per_base = dot_nn(base_hot, t0) + dot_nn(base_hot, t1) + dot_nn(base_hot, t2)
    b0, b1, b2 = split3(per_base)
    one = jnp.ones((8, samples), BF)
    s0, s1, s2 = [s.astype(F32) for s in split3(dot_nt(one, b0) + dot_nt(one, b1) + dot_nt(one, b2))]
    count = dot_nt(jnp.ones((8, blocks), BF), base_hot)
    r8 = iota((8, LANES), 0)
    own_rows = jnp.where(r8 == 1, s0, jnp.where(r8 == 2, s1, jnp.where(r8 == 3, s2, count)))
    for o in range(n_pix):
        cols = slice(o * LANES, (o + 1) * LANES)
        tile = jnp.where(r8 == 0, where[:, cols], own_rows).astype(BF)
        for d in range(n_det):
            to, rows = d * n_pix + o, slice(d * half, (d + 1) * half)
            give_ref[to] = theirs[rows, cols].astype(BF)
            mine_ref[to] = mine[rows, cols]
            rest_ref[to, 0:half, :] = columns[rows, cols]
            rest_ref[to, half:, :] = tile


def add_kernel(mine_ref, took_ref, rest_ref, send_ref):
    rows, half, _ = mine_ref.shape
    for g in range(rows):
        send_ref[g, 0:half, :] = rest_ref[g, 0:half, :]
        send_ref[g, half : 2 * half, :] = (mine_ref[g] + took_ref[g].astype(F32)).astype(BF)
        send_ref[g, 2 * half :, :] = rest_ref[g, half:, :]


def project(col_t, sky_t, pb_hot, base_hot, row_hot):
    spread = dot_nn(sky_t.astype(BF), pb_hot)
    per_slot = jnp.sum(col_t.astype(F32) * spread, axis=0, keepdims=True)
    parts = [jnp.where(row_hot, p.astype(F32), 0.0).astype(BF) for p in split3(per_slot)]
    return dot_nt(parts[0], base_hot) + dot_nt(parts[1], base_hot) + dot_nt(parts[2], base_hot)


def bin_amps(amps, col_t, pb_hot, base_hot, row_hot):
    a0, a1, a2 = split3(amps)
    spread = dot_nn(a0, base_hot) + dot_nn(a1, base_hot) + dot_nn(a2, base_hot)
    per_slot = jnp.sum(jnp.where(row_hot, spread, 0.0), axis=0, keepdims=True)
    terms = col_t.astype(F32) * per_slot
    high = terms.astype(BF)
    low = (terms - high.astype(F32)).astype(BF)
    return dot_nt(high, pb_hot) + dot_nt(low, pb_hot)


def hots(idx_ref):
    slots = idx_ref.shape[1]
    pb_hot = (iota((PB_DEV, slots), 0).astype(F32) == idx_ref[0:1, :]).astype(F32).astype(BF)
    base_hot = (iota((NBASE_DEV, slots), 0).astype(F32) == idx_ref[1:2, :]).astype(F32).astype(BF)
    return pb_hot, base_hot


def row_mask(rows, slots):
    return iota((rows, slots), 1) // CAP == iota((rows, slots), 0)


def owner_kernel(pch, n_pix, got_ref, send_ref, col_ref, idx_ref, inv_ref, base_ref, count_ref):
    rows = got_ref.shape[0]
    half = pch // 2
    low = iota((half, LANES), 1) < CAP
    low8 = iota((8, LANES), 1) < CAP
    maps = [jnp.zeros((half, LANES), F32), jnp.zeros((half, LANES), F32)]
    for g in range(rows):
        core = (g // n_pix) % 2
        maps[core] = maps[core] + got_ref[g, half : 2 * half, :].astype(F32)
    for i in range(rows // 2):
        a, b = got_ref[2 * i, 0:half, :].astype(F32), got_ref[2 * i + 1, 0:half, :].astype(F32)
        cols = slice(i * LANES, (i + 1) * LANES)
        col_ref[0:half, cols] = jnp.where(low, a, pltpu.roll(b, CAP, 1)).astype(BF)
        col_ref[half:, cols] = jnp.where(low, pltpu.roll(a, CAP, 1), b).astype(BF)
        ta, tb = got_ref[2 * i, 2 * half :, :].astype(F32), got_ref[2 * i + 1, 2 * half :, :].astype(F32)
        pb = jnp.where(low8, ta, pltpu.roll(tb, CAP, 1))
        base = jnp.where(low8, pltpu.roll(ta, CAP, 1), tb)
        idx_ref[0:1, cols] = pb[0:1]
        idx_ref[1:2, cols] = base[0:1]
        for g, t in ((2 * i, ta), (2 * i + 1, tb)):
            base_ref[g : g + 1, :] = t[1:2] + t[2:3] + t[3:4]
            count_ref[g : g + 1, :] = t[4:5]
    maps = jnp.concatenate(maps, axis=0)
    inv = 1.0 / (maps[:, 0:PB_DEV] + 1.0)
    inv_ref[...] = inv
    sky = maps[:, PB_DEV:] * inv
    pb_hot, base_hot = hots(idx_ref)
    part = project(col_ref[...], sky, pb_hot, base_hot, row_mask(rows, col_ref.shape[1])).astype(BF)
    for g in range(rows):
        send_ref[g] = part


def total_of(got_ref):
    acc = got_ref[0].astype(F32)
    for g in range(1, got_ref.shape[0]):
        acc = acc + got_ref[g].astype(F32)
    return acc


def first_kernel(samples, got_ref, col_ref, idx_ref, inv_ref, base_ref, send_ref, rhs_ref):
    rhs = (base_ref[...] - total_of(got_ref)) * (1.0 / samples)
    rhs_ref[...] = rhs
    pb_hot, base_hot = hots(idx_ref)
    row_hot = row_mask(rhs.shape[0], col_ref.shape[1])
    binned = bin_amps(rhs, col_ref[...], pb_hot, base_hot, row_hot)
    part = project(col_ref[...], binned * inv_ref[...], pb_hot, base_hot, row_hot).astype(BF)
    for g in range(send_ref.shape[0]):
        send_ref[g] = part


def second_kernel(samples, got_ref, col_ref, idx_ref, inv_ref, rhs_ref, count_ref, send_ref, state_ref):
    rhs = rhs_ref[...]
    more = count_ref[...] + 1.0
    image = more * rhs - total_of(got_ref) * (1.0 / samples)
    rr = jnp.sum(rhs * rhs)
    alpha = rr / jnp.sum(rhs * image)
    levels = alpha * rhs
    error = rhs - alpha * image
    new = jnp.sum(error * error)
    heading = error + (new / rr) * rhs
    curve = jnp.sum(more * heading * heading)
    pb_hot, base_hot = hots(idx_ref)
    rows = rhs.shape[0]
    row_hot = row_mask(rows, col_ref.shape[1])
    binned = bin_amps(heading, col_ref[...], pb_hot, base_hot, row_hot)
    sky = binned * inv_ref[...]
    quad = jnp.sum(binned * sky)
    part = project(col_ref[...], sky, pb_hot, base_hot, row_hot)
    for g in range(rows):
        send_ref[g, 0:1, 0:LANES] = part[g : g + 1]
        send_ref[g, 0:1, LANES:] = jnp.full((1, LANES), quad, F32)
    state_ref[0] = levels
    state_ref[1] = error
    state_ref[2] = heading
    state_ref[3] = more * heading
    state_ref[4] = jnp.full((rows, LANES), new, F32)
    state_ref[5] = jnp.full((rows, LANES), curve, F32)


def last_kernel(samples, n_pix, got_ref, state_ref, levels_ref, error_ref):
    me = lax.axis_index("det") * n_pix + lax.axis_index("pix")
    acc = got_ref[0]
    for g in range(1, got_ref.shape[0]):
        acc = acc + got_ref[g]
    acc = acc * (1.0 / samples)
    mine = [state_ref[k, pl.ds(me, 1), :] for k in range(6)]
    levels, error, heading, scaled, new, curve = mine
    image = scaled - acc[:, 0:LANES]
    alpha = new / (curve - acc[:, LANES:])
    levels_ref[...] = levels + alpha * heading
    error_ref[...] = error - alpha * image


def call(kernel, outs, *args, **kw):
    vmem = pl.BlockSpec(memory_space=pltpu.VMEM)
    return pl.pallas_call(
        kernel,
        out_shape=outs,
        in_specs=[vmem] * len(args),
        out_specs=[vmem] * len(outs),
        compiler_params=pltpu.CompilerParams(vmem_limit_bytes=VMEM_LIMIT),
        **kw,
    )(*args)


def exchange(x):
    return lax.all_to_all(x, AXES, split_axis=0, concat_axis=0, tiled=True)


def body(timestream, weights, block_owner, block_local, baseline_of):
    n_det, n_pix = lax.axis_size("det"), lax.axis_size("pix")
    rows = n_det * n_pix
    _, blocks, samples, pixels = weights.shape
    pch = pixels // n_det
    half = pch // 2
    slots = rows * CAP
    group = 32
    shape = jax.ShapeDtypeStruct
    here = pl.BlockSpec(memory_space=pltpu.VMEM)
    wide = n_pix * LANES
    mine, give, rest = pl.pallas_call(
        functools.partial(bin_kernel, n_det, n_pix, group),
        out_shape=[shape((rows, half, LANES), F32), shape((rows, half, LANES), BF), shape((rows, half + 8, LANES), BF)],
        in_specs=[pl.BlockSpec(memory_space=pltpu.HBM)] * 5,
        out_specs=[here] * 3,
        scratch_shapes=[
            pltpu.VMEM((blocks, samples, pixels), BF),
            pltpu.VMEM((1, blocks, samples), F32),
            *[pltpu.VMEM((1, blocks), jnp.int32)] * 3,
            *[pltpu.VMEM((blocks, pixels), F32)] * 3,
            *[pltpu.VMEM((blocks, wide), BF)] * 4,
            pltpu.SemaphoreType.DMA((blocks // group,)),
            pltpu.SemaphoreType.DMA((4,)),
        ],
        compiler_params=pltpu.CompilerParams(vmem_limit_bytes=VMEM_LIMIT),
    )(timestream, weights, block_owner.reshape(1, blocks), block_local, baseline_of)
    took = lax.ppermute(give, "det", [(i, i ^ 1) for i in range(n_det)])
    sent = call(add_kernel, [shape((rows, pch + 8, LANES), BF)], mine, took, rest)[0]
    got = exchange(sent)
    everyone = shape((rows, rows, NBASE_DEV), BF)
    vector = shape((rows, NBASE_DEV), F32)
    part, col_t, idx, inv, base, count = call(
        functools.partial(owner_kernel, pch, n_pix),
        [everyone, shape((pch, slots), BF), shape((8, slots), F32), shape((pch, PB_DEV), F32), vector, vector],
        got,
    )
    part, rhs = call(
        functools.partial(first_kernel, samples), [everyone, vector], exchange(part), col_t, idx, inv, base
    )
    part, state = call(
        functools.partial(second_kernel, samples),
        [shape((rows, 1, 2 * LANES), F32), shape((6, rows, NBASE_DEV), F32)],
        exchange(part), col_t, idx, inv, rhs, count,
    )
    own = shape((1, NBASE_DEV), F32)
    return tuple(call(functools.partial(last_kernel, samples, n_pix), [own, own], exchange(part), state))


def solution(mesh):
    placed = (
        P(AXES, None, None),
        P(AXES, None, None, None),
        P(AXES, None, None),
        P(AXES, None),
        P(AXES, None),
    )
    return jax.shard_map(
        body,
        mesh=mesh,
        in_specs=placed,
        out_specs=(P(AXES, None), P(AXES, None)),
        check_vma=False,
    )
```

```python
import functools

import jax
import jax.numpy as jnp
from jax import lax
from jax.experimental import pallas as pl
from jax.experimental.pallas import tpu as pltpu
from jax.sharding import PartitionSpec as P

PB_DEV = 64
NBASE_DEV = 128
CAP = 64
LANES = 128
AXES = ("det", "pix")
BF = jnp.bfloat16
F32 = jnp.float32
VMEM_LIMIT = 48 * 1024 * 1024


def dot_nn(a, b):
    return lax.dot_general(a, b, (((1,), (0,)), ((), ())), preferred_element_type=F32)


def dot_nt(a, b):
    return lax.dot_general(a, b, (((1,), (1,)), ((), ())), preferred_element_type=F32)


def split3(v):
    a = v.astype(BF)
    left = v - a.astype(F32)
    b = left.astype(BF)
    c = (left - b.astype(F32)).astype(BF)
    return a, b, c


def iota(shape, dim):
    return lax.broadcasted_iota(jnp.int32, shape, dim)


def column(row):
    n = row.shape[1]
    eye = (iota((n, n), 0) == iota((n, n), 1)).astype(F32).astype(BF)
    return dot_nt(eye, jnp.broadcast_to(row.astype(F32).astype(BF), (8, n)))[:, 0:1].astype(jnp.int32)


def hot(target, wide):
    return (iota((target.shape[0], wide), 1) == target).astype(F32).astype(BF)


def bin_kernel(
    n_det, n_pix, group, ts_hbm, w_hbm, own_hbm, loc_hbm,
    give_ref, hit_ref, dat_ref, col_ref, pb_hot,
    w_s, ts_s, own_s, loc_s, hit_s, dat_s, col_s, sem, small,
):
    blocks, samples, pixels = w_s.shape
    steps = blocks // group

    def weights(c):
        where = pl.ds(c * group, group)
        return pltpu.make_async_copy(w_hbm.at[0, where], w_s.at[where], sem.at[c])

    def series(c):
        where = pl.ds(c * group, group)
        return pltpu.make_async_copy(ts_hbm.at[0, where], ts_s.at[0, where], small.at[c])

    indices = [
        pltpu.make_async_copy(src, dst, small.at[steps + k]) for k, (src, dst) in enumerate(((own_hbm, own_s), (loc_hbm, loc_s)))
    ]
    for copy in indices:
        copy.start()
    for c in range(steps):
        series(c).start()
        weights(c).start()
    row = iota((8, samples), 0)
    place = iota((samples, LANES), 1)

    def row_sums(c):
        acc = jnp.zeros((samples, LANES), F32)
        for j in range(group):
            w = w_s[c * group + j].astype(F32)
            halves = w[:, 0:LANES]
            for k in range(LANES, pixels, LANES):
                halves = halves + w[:, k : k + LANES]
            acc = jnp.where(place == j, jnp.sum(halves, axis=1, keepdims=True), acc)
        return acc.T[0:group]

    def terms(c, sums):
        for j in range(group):
            r = jnp.broadcast_to(sums[j : j + 1], (8, samples))
            u = jnp.broadcast_to(ts_s[0, pl.ds(c * group + j, 1), :], (8, samples))
            lhs = jnp.where(row == 0, r, jnp.where(row == 1, u, 1.0)).astype(BF)
            t = dot_nn(lhs, w_s[c * group + j])
            where = pl.ds(c * group + j, 1)
            hit_s[where, :] = t[0:1]
            dat_s[where, :] = t[1:2]
            col_s[where, :] = t[2:3]

    def step(c, sums):
        series(c - 1).wait()
        weights(c).wait()
        after = row_sums(c)
        terms(c - 1, sums)
        return after

    weights(0).wait()
    sums = lax.fori_loop(1, steps, step, row_sums(0))
    series(steps - 1).wait()
    for copy in indices:
        copy.wait()
    pb_hot[...] = hot(column(own_s[...]) * PB_DEV + column(loc_s[...]), n_pix * PB_DEV)
    terms(steps - 1, sums)
    hit_ref[...] = hit_s[...].T
    dat_ref[...] = dat_s[...].T
    col_ref[...] = col_s[...].T
    core = lax.rem(lax.axis_index("det"), 2)
    binned(n_det, n_pix, 1 - core, hit_ref, dat_ref, pb_hot, give_ref)


def pair(first, second, swap):
    low = iota(first.shape, 1) < CAP
    return jnp.where(low, first, swap(second)), jnp.where(low, swap(first), second)


def swap_halves(v):
    return pltpu.roll(v, CAP, 1)


def two_up(n_det, n_pix, first, second, ref):
    half = first.shape[0] // n_det
    for i in range(n_pix // 2):
        cols = slice(i * LANES, (i + 1) * LANES)
        for o, tile in zip((2 * i, 2 * i + 1), pair(first[:, cols], second[:, cols], swap_halves)):
            tile = tile.astype(ref.dtype)
            for d in range(n_det):
                ref[d * n_pix + o, 0:half, :] = tile[d * half : (d + 1) * half]


def binned(n_det, n_pix, which, hit_ref, dat_ref, pb_hot, ref):
    half = hit_ref.shape[0] // n_det // 2
    rows = [
        of[pl.ds(pl.multiple_of((2 * d + which) * half, half), half), :].astype(BF) for of in (hit_ref, dat_ref) for d in range(n_det)
    ]
    both = dot_nn(jnp.concatenate(rows, axis=0), pb_hot[...])
    two_up(n_det, n_pix, both[: n_det * half], both[n_det * half :], ref)


def fill_kernel(n_det, n_pix, ts_ref, own_ref, loc_ref, base_ref, hit_ref, dat_ref, col_ref, pb_hot, mine_ref, rest_ref):
    _, blocks, samples = ts_ref.shape
    own = column(own_ref[...])
    tri = (iota((blocks, blocks), 1) < iota((blocks, blocks), 0)).astype(F32).astype(BF)
    own_hot = (own == iota((blocks, LANES), 1)).astype(F32)
    before = dot_nn(tri, own_hot.astype(BF))
    slot = own * CAP + jnp.sum(before * own_hot, axis=1, keepdims=True).astype(jnp.int32)
    slot_hot = hot(slot, n_pix * CAP)
    core = lax.rem(lax.axis_index("det"), 2)
    binned(n_det, n_pix, core, hit_ref, dat_ref, pb_hot, mine_ref)
    col_t = col_ref[...].astype(BF)
    pch = col_t.shape[0] // n_det
    half = pch // 2
    rows = [col_t[(2 * d + k) * half : (2 * d + k + 1) * half] for k in (0, 1) for d in range(n_det)]
    both = dot_nn(jnp.concatenate(rows, axis=0), slot_hot)
    two_up(n_det, n_pix, both[: n_det * half], both[n_det * half :], rest_ref)

    sums = jnp.sum(ts_ref[0].T, axis=0, keepdims=True)
    w0, w1, w2 = [w.astype(F32) for w in split3(sums / jnp.sum(col_t.astype(F32), axis=0, keepdims=True))]
    r16 = iota((16, blocks), 0)
    lhs = jnp.where(r16 == 0, loc_ref[...].astype(F32), jnp.where(r16 == 8, base_ref[...].astype(F32), 0.0))
    lhs = jnp.where(r16 == 1, w0, jnp.where(r16 == 9, w1, jnp.where(r16 == 2, w2, lhs)))
    where = dot_nn(lhs.astype(BF), slot_hot)
    base_hot = (column(base_ref[...]) == iota((blocks, NBASE_DEV), 1)).astype(F32)
    count = jnp.sum(base_hot, axis=0, keepdims=True)
    r8 = iota((8, LANES), 0)
    for i in range(n_pix // 2):
        cols = slice(i * LANES, (i + 1) * LANES)
        for o, tile in zip((2 * i, 2 * i + 1), pair(where[0:8, cols], where[8:16, cols], swap_halves)):
            tile = jnp.where(r8 == 3, count, tile).astype(BF)
            for d in range(n_det):
                rest_ref[d * n_pix + o, half:, :] = tile


def join_kernel(mine_ref, took_ref, rest_ref, send_ref):
    rows, half, _ = mine_ref.shape
    for g in range(rows):
        send_ref[g, 0:half, :] = rest_ref[g, 0:half, :]
        send_ref[g, half : 2 * half, :] = (mine_ref[g] + took_ref[g].astype(F32)).astype(BF)
        send_ref[g, 2 * half :, :] = rest_ref[g, half:, :]


def split2(v):
    a = v.astype(BF)
    return a, (v - a.astype(F32)).astype(BF)


def total(v):
    return jnp.sum(jnp.sum(v, axis=0, keepdims=True), axis=1, keepdims=True)


def project(col_t, sky_t, pb_hot, base_hot, row_hot, shift=None):
    rows = row_hot.shape[0]
    spread = dot_nn(sky_t.astype(BF), pb_hot)
    spread = spread if shift is None else spread - shift
    per_slot = jnp.sum(col_t.astype(F32) * spread, axis=0, keepdims=True)
    parts = [jnp.where(row_hot, p.astype(F32), 0.0).astype(BF) for p in split2(per_slot)]
    both = dot_nt(jnp.concatenate(parts, axis=0), base_hot)
    return both[0:rows] + both[rows:]


def bin_amps(amps, col_t, pb_hot, base_hot, row_hot):
    rows = row_hot.shape[0]
    both = dot_nn(jnp.concatenate(split2(amps), axis=0), base_hot)
    per_slot = jnp.sum(jnp.where(row_hot, both[0:rows] + both[rows:], 0.0), axis=0, keepdims=True)
    pch = col_t.shape[0]
    both = dot_nt(jnp.concatenate(split2(col_t.astype(F32) * per_slot), axis=0), pb_hot)
    return both[0:pch] + both[pch:]


def row_mask(rows, slots):
    return iota((rows, slots), 1) // CAP == iota((rows, slots), 0)


def halves_out(part, keep_ref, give_ref, work):
    work[...] = part
    half = keep_ref.shape[0]
    core = lax.rem(lax.axis_index("det"), 2)
    keep_ref[...] = work[pl.ds(pl.multiple_of(core * half, half), half), :]
    give_ref[...] = work[pl.ds(pl.multiple_of((1 - core) * half, half), half), :]


def sum_kernel(keep_ref, took_ref, send_ref):
    part = (keep_ref[...] + took_ref[...]).astype(BF)
    for g in range(send_ref.shape[0]):
        send_ref[g] = part


def total_of(got_ref, n_pix):
    sums = [None, None]
    for g in range(got_ref.shape[0]):
        core = (g // n_pix) % 2
        term = got_ref[g].astype(F32)
        sums[core] = term if sums[core] is None else sums[core] + term
    return jnp.concatenate(sums, axis=0)


def columns_of(pack_ref):
    slots = pack_ref.shape[1] - LANES
    inv = pack_ref[:, slots:].astype(F32)
    return pack_ref[:, :slots], inv[:, 0:PB_DEV] + inv[:, PB_DEV:]


def owner_kernel(pch, n_pix, got_ref, keep_ref, give_ref, pack_ref, pb_ref, hot_ref, more_ref, work, mean):
    rows = got_ref.shape[0]
    half = pch // 2
    slots = rows * CAP
    pb_of = iota((PB_DEV, LANES), 0).astype(F32)
    base_of = iota((NBASE_DEV, LANES), 0).astype(F32)
    maps = [jnp.zeros((half, LANES), F32), jnp.zeros((half, LANES), F32)]
    for g in range(rows):
        core = (g // n_pix) % 2
        maps[core] = maps[core] + got_ref[g, half : 2 * half, :].astype(F32)
    for i in range(rows // 2):
        cols = slice(i * LANES, (i + 1) * LANES)
        halves = pair(got_ref[2 * i, 0:half, :].astype(F32), got_ref[2 * i + 1, 0:half, :].astype(F32), swap_halves)
        pack_ref[0:half, cols] = halves[0].astype(BF)
        pack_ref[half:, cols] = halves[1].astype(BF)
        tiles = [got_ref[2 * i + k, 2 * half :, :].astype(F32) for k in (0, 1)]
        one, two = pair(*tiles, swap_halves)
        pb_ref[:, cols] = (pb_of == one[0:1]).astype(F32).astype(BF)
        hot_ref[:, cols] = (base_of == two[0:1]).astype(F32).astype(BF)
        mean[0:1, cols] = one[1:2] + two[1:2] + one[2:3]
        for k in (0, 1):
            more_ref[2 * i + k : 2 * i + k + 1, :] = tiles[k][3:4] + 1.0
    maps = jnp.concatenate(maps, axis=0)
    inv = 1.0 / (maps[:, 0:PB_DEV] + 1.0)
    pack_ref[:, slots:] = jnp.concatenate([v.astype(F32) for v in split2(inv)], axis=1).astype(BF)
    sky = maps[:, PB_DEV:] * inv
    part = project(pack_ref[:, :slots], sky, pb_ref[...], hot_ref[...], row_mask(rows, slots), mean[0:1, :])
    halves_out(part, keep_ref, give_ref, work)


def first_kernel(samples, n_pix, got_ref, pack_ref, other_ref, pb_ref, hot_ref, send_ref, rhs_ref):
    rhs = total_of(got_ref, n_pix) * (-1.0 / samples)
    rhs_ref[...] = rhs
    rows = rhs.shape[0]
    slots = rows * CAP
    columns, inv = zip(columns_of(pack_ref), columns_of(other_ref))
    binned = bin_amps(rhs, jnp.concatenate(columns, axis=0), pb_ref[...], hot_ref[...], row_mask(rows, slots))
    sky = binned * jnp.concatenate(inv, axis=0)
    core = lax.rem(lax.axis_index("det"), 2)
    mine = pl.ds(pl.multiple_of(core * (slots // 2), slots // 2), slots // 2)
    columns = jnp.concatenate([pack_ref[:, mine], other_ref[:, mine]], axis=0)
    part = project(columns, sky, pb_ref[:, mine], hot_ref[:, mine], row_mask(rows // 2, slots // 2)).astype(BF)
    for g in range(rows):
        send_ref[g] = part


def second_kernel(samples, n_pix, got_ref, pack_ref, pb_ref, hot_ref, rhs_ref, more_ref, send_ref, state_ref):
    rhs = rhs_ref[...]
    more = more_ref[...]
    image = more * rhs - total_of(got_ref, n_pix) * (1.0 / samples)
    rr = total(rhs * rhs)
    alpha = rr / total(rhs * image)
    error = rhs - alpha * image
    new = total(error * error)
    heading = error + (new / rr) * rhs
    rows = rhs.shape[0]
    columns, inv = columns_of(pack_ref)
    row_hot = row_mask(rows, columns.shape[1])
    binned = bin_amps(heading, columns, pb_ref[...], hot_ref[...], row_hot)
    sky = binned * inv
    part = project(columns, sky, pb_ref[...], hot_ref[...], row_hot)
    quad = jnp.broadcast_to(total(binned * sky), (1, LANES))
    for g in range(rows):
        send_ref[g, 0:1, 0:LANES] = part[g : g + 1]
        send_ref[g, 0:1, LANES:] = quad
    scaled = more * heading
    state_ref[0] = alpha * rhs
    state_ref[1] = error
    state_ref[2] = heading
    state_ref[3] = scaled
    state_ref[4] = jnp.broadcast_to(new, (rows, LANES))
    state_ref[5] = jnp.broadcast_to(total(scaled * heading), (rows, LANES))


def last_kernel(samples, n_pix, got_ref, state_ref, levels_ref, error_ref):
    me = lax.axis_index("det") * n_pix + lax.axis_index("pix")
    acc = got_ref[0]
    for g in range(1, got_ref.shape[0]):
        acc = acc + got_ref[g]
    acc = acc * (1.0 / samples)
    mine = [state_ref[k, pl.ds(me, 1), :] for k in range(6)]
    levels, error, heading, scaled, new, curve = mine
    image = scaled - acc[:, 0:LANES]
    alpha = new / (curve - acc[:, LANES:])
    levels_ref[...] = levels + alpha * heading
    error_ref[...] = error - alpha * image


def call(kernel, outs, *args, scratch=()):
    vmem = pl.BlockSpec(memory_space=pltpu.VMEM)
    return pl.pallas_call(
        kernel,
        out_shape=outs,
        in_specs=[vmem] * len(args),
        out_specs=[vmem] * len(outs),
        scratch_shapes=scratch,
        compiler_params=pltpu.CompilerParams(vmem_limit_bytes=VMEM_LIMIT),
        cost_estimate=pl.CostEstimate(flops=10**8, bytes_accessed=4 * 10**6, transcendentals=0),
    )(*args)


def exchange(x):
    return lax.all_to_all(x, AXES, split_axis=0, concat_axis=0, tiled=True)


def other_core(x):
    return lax.ppermute(x, "det", [(i, i ^ 1) for i in range(lax.axis_size("det"))])


def body(timestream, weights, block_owner, block_local, baseline_of):
    n_det, n_pix = lax.axis_size("det"), lax.axis_size("pix")
    rows = n_det * n_pix
    _, blocks, samples, pixels = weights.shape
    pch = pixels // n_det
    half = pch // 2
    slots = rows * CAP
    group = 32
    shape = jax.ShapeDtypeStruct
    hbm = functools.partial(pltpu.with_memory_space_constraint, memory_space=pltpu.HBM)
    owners = block_owner.reshape(1, blocks)
    give, *filling = pl.pallas_call(
        functools.partial(bin_kernel, n_det, n_pix, group),
        out_shape=[
            shape((rows, half, LANES), BF),
            *[shape((pixels, blocks), F32)] * 3,
            shape((blocks, n_pix * PB_DEV), BF),
        ],
        in_specs=[pl.BlockSpec(memory_space=pltpu.HBM)] * 4,
        out_specs=[pl.BlockSpec(memory_space=pltpu.VMEM)] * 5,
        scratch_shapes=[
            pltpu.VMEM((blocks, samples, pixels), BF),
            pltpu.VMEM((1, blocks, samples), F32),
            *[pltpu.VMEM((1, blocks), jnp.int32)] * 2,
            *[pltpu.VMEM((blocks, pixels), F32)] * 3,
            pltpu.SemaphoreType.DMA((blocks // group,)),
            pltpu.SemaphoreType.DMA((blocks // group + 2,)),
        ],
        compiler_params=pltpu.CompilerParams(vmem_limit_bytes=VMEM_LIMIT),
        cost_estimate=pl.CostEstimate(flops=10**8, bytes_accessed=2**25, transcendentals=0),
    )(hbm(timestream), weights, hbm(owners), hbm(block_local))
    took = other_core(give)
    mine, rest = call(
        functools.partial(fill_kernel, n_det, n_pix),
        [shape((rows, half, LANES), F32), shape((rows, half + 8, LANES), BF)],
        timestream, owners, block_local, baseline_of, *filling,
    )
    got = exchange(call(join_kernel, [shape((rows, pch + 8, LANES), BF)], mine, took, rest)[0])
    vector = shape((rows, NBASE_DEV), F32)
    part = shape((rows // 2, NBASE_DEV), F32)

    everyone = shape((rows, rows // 2, NBASE_DEV), BF)
    keep, give, pack, pb_hot, base_hot, more = call(
        functools.partial(owner_kernel, pch, n_pix),
        [part, part, shape((pch, slots + LANES), BF), shape((PB_DEV, slots), BF), shape((NBASE_DEV, slots), BF), vector],
        got,
        scratch=[pltpu.VMEM((rows, NBASE_DEV), F32), pltpu.VMEM((8, slots), F32)],
    )
    took, pack = lax.optimization_barrier((other_core(give), pack))
    other = other_core(pack)
    sent = call(sum_kernel, [everyone], keep, took)[0]
    sent, rhs = call(
        functools.partial(first_kernel, samples, n_pix), [everyone, vector], exchange(sent), pack, other, pb_hot, base_hot
    )
    sent, state = call(
        functools.partial(second_kernel, samples, n_pix),
        [shape((rows, 1, 2 * LANES), F32), shape((6, rows, NBASE_DEV), F32)],
        exchange(sent), pack, pb_hot, base_hot, rhs, more,
    )
    own = shape((1, NBASE_DEV), F32)
    return tuple(call(functools.partial(last_kernel, samples, n_pix), [own, own], exchange(sent), state))


def solution(mesh):
    placed = (
        P(AXES, None, None),
        P(AXES, None, None, None),
        P(AXES, None, None),
        P(AXES, None),
        P(AXES, None),
    )
    return jax.shard_map(
        body,
        mesh=mesh,
        in_specs=placed,
        out_specs=(P(AXES, None), P(AXES, None)),
        check_vma=False,
    )
```

```python
import functools

import jax
import jax.numpy as jnp
from jax import lax
from jax.experimental import pallas as pl
from jax.experimental.pallas import tpu as pltpu
from jax.sharding import PartitionSpec as P

PB_DEV = 64
NBASE_DEV = 128
CAP = 64
LANES = 128
AXES = ("det", "pix")
BF = jnp.bfloat16
F32 = jnp.float32
VMEM_LIMIT = 48 * 1024 * 1024


def dot_nn(a, b):
    return lax.dot_general(a, b, (((1,), (0,)), ((), ())), preferred_element_type=F32)


def dot_nt(a, b):
    return lax.dot_general(a, b, (((1,), (1,)), ((), ())), preferred_element_type=F32)


def split3(v):
    a = v.astype(BF)
    left = v - a.astype(F32)
    b = left.astype(BF)
    c = (left - b.astype(F32)).astype(BF)
    return a, b, c


def iota(shape, dim):
    return lax.broadcasted_iota(jnp.int32, shape, dim)


def column(row):
    n = row.shape[1]
    eye = (iota((n, n), 0) == iota((n, n), 1)).astype(F32).astype(BF)
    return dot_nt(eye, jnp.broadcast_to(row.astype(F32).astype(BF), (8, n)))[:, 0:1].astype(jnp.int32)


def hot(target, wide):
    return (iota((target.shape[0], wide), 1) == target).astype(F32).astype(BF)


def bin_kernel(
    n_det, n_pix, group, ts_hbm, w_hbm, own_hbm, loc_hbm,
    give_ref, hit_ref, dat_ref, col_ref, pb_hot,
    w_s, ts_s, own_s, loc_s, hit_s, dat_s, col_s, sem, small,
):
    blocks, samples, pixels = w_s.shape
    steps = blocks // group - 1
    short = group // 2

    def copies(first, many, k):
        where = pl.ds(first, many)
        return (
            pltpu.make_async_copy(ts_hbm.at[0, where], ts_s.at[0, where], small.at[k]),
            pltpu.make_async_copy(w_hbm.at[0, where], w_s.at[where], sem.at[k]),
        )

    def full(c):
        return copies(c * group, group, c)

    ends = [copies(steps * group + k * short, short, steps + k) for k in (0, 1)]

    indices = [
        pltpu.make_async_copy(src, dst, small.at[steps + 2 + k]) for k, (src, dst) in enumerate(((own_hbm, own_s), (loc_hbm, loc_s)))
    ]
    for copy in indices:
        copy.start()
    for piece in [full(c) for c in range(steps)] + ends:
        for copy in piece:
            copy.start()
    row = iota((8, samples), 0)
    place = iota((samples, LANES), 1)

    def row_sums(first, many):
        acc = jnp.zeros((samples, LANES), F32)
        for j in range(many):
            w = w_s[first + j].astype(F32)
            halves = w[:, 0:LANES]
            for k in range(LANES, pixels, LANES):
                halves = halves + w[:, k : k + LANES]
            acc = jnp.where(place == j, jnp.sum(halves, axis=1, keepdims=True), acc)
        return acc.T[0:many]

    def terms(first, many, sums):
        for j in range(many):
            r = jnp.broadcast_to(sums[j : j + 1], (8, samples))
            u = jnp.broadcast_to(ts_s[0, pl.ds(first + j, 1), :], (8, samples))
            lhs = jnp.where(row == 0, r, jnp.where(row == 1, u, 1.0)).astype(BF)
            t = dot_nn(lhs, w_s[first + j])
            where = pl.ds(first + j, 1)
            hit_s[where, :] = t[0:1]
            dat_s[where, :] = t[1:2]
            col_s[where, :] = t[2:3]

    def wait(piece):
        for copy in piece:
            copy.wait()

    def step(c, sums):
        wait(full(c))
        after = row_sums(c * group, group)
        terms((c - 1) * group, group, sums)
        return after

    wait(full(0))
    sums = lax.fori_loop(1, steps, step, row_sums(0, group))
    wait(ends[0])
    after = row_sums(steps * group, short)
    terms((steps - 1) * group, group, sums)
    wait(ends[1])
    last = row_sums(steps * group + short, short)
    terms(steps * group, short, after)
    for copy in indices:
        copy.wait()
    pb_hot[...] = hot(column(own_s[...]) * PB_DEV + column(loc_s[...]), n_pix * PB_DEV)
    terms(steps * group + short, short, last)
    hit_ref[...] = hit_s[...].T
    dat_ref[...] = dat_s[...].T
    col_ref[...] = col_s[...].T
    core = lax.rem(lax.axis_index("det"), 2)
    binned(n_det, n_pix, 1 - core, hit_ref, dat_ref, pb_hot, give_ref)


def pair(first, second, swap):
    low = iota(first.shape, 1) < CAP
    return jnp.where(low, first, swap(second)), jnp.where(low, swap(first), second)


def swap_halves(v):
    return pltpu.roll(v, CAP, 1)


def two_up(n_det, n_pix, first, second, ref):
    half = first.shape[0] // n_det
    for i in range(n_pix // 2):
        cols = slice(i * LANES, (i + 1) * LANES)
        for o, tile in zip((2 * i, 2 * i + 1), pair(first[:, cols], second[:, cols], swap_halves)):
            tile = tile.astype(ref.dtype)
            for d in range(n_det):
                ref[d * n_pix + o, 0:half, :] = tile[d * half : (d + 1) * half]


def binned(n_det, n_pix, which, hit_ref, dat_ref, pb_hot, ref):
    half = hit_ref.shape[0] // n_det // 2
    rows = [
        of[pl.ds(pl.multiple_of((2 * d + which) * half, half), half), :].astype(BF) for of in (hit_ref, dat_ref) for d in range(n_det)
    ]
    both = dot_nn(jnp.concatenate(rows, axis=0), pb_hot[...])
    two_up(n_det, n_pix, both[: n_det * half], both[n_det * half :], ref)


def fill_kernel(n_det, n_pix, ts_ref, own_ref, loc_ref, base_ref, hit_ref, dat_ref, col_ref, pb_hot, mine_ref, rest_ref):
    _, blocks, samples = ts_ref.shape
    own = column(own_ref[...])
    tri = (iota((blocks, blocks), 1) < iota((blocks, blocks), 0)).astype(F32).astype(BF)
    own_hot = (own == iota((blocks, LANES), 1)).astype(F32)
    before = dot_nn(tri, own_hot.astype(BF))
    slot = own * CAP + jnp.sum(before * own_hot, axis=1, keepdims=True).astype(jnp.int32)
    slot_hot = hot(slot, n_pix * CAP)
    core = lax.rem(lax.axis_index("det"), 2)
    binned(n_det, n_pix, core, hit_ref, dat_ref, pb_hot, mine_ref)
    col_t = col_ref[...].astype(BF)
    pch = col_t.shape[0] // n_det
    half = pch // 2
    rows = [col_t[(2 * d + k) * half : (2 * d + k + 1) * half] for k in (0, 1) for d in range(n_det)]
    both = dot_nn(jnp.concatenate(rows, axis=0), slot_hot)
    two_up(n_det, n_pix, both[: n_det * half], both[n_det * half :], rest_ref)

    sums = jnp.sum(ts_ref[0].T, axis=0, keepdims=True)
    w0, w1, w2 = [w.astype(F32) for w in split3(sums / jnp.sum(col_t.astype(F32), axis=0, keepdims=True))]
    r16 = iota((16, blocks), 0)
    lhs = jnp.where(r16 == 0, loc_ref[...].astype(F32), jnp.where(r16 == 8, base_ref[...].astype(F32), 0.0))
    lhs = jnp.where(r16 == 1, w0, jnp.where(r16 == 9, w1, jnp.where(r16 == 2, w2, lhs)))
    where = dot_nn(lhs.astype(BF), slot_hot)
    base_hot = (column(base_ref[...]) == iota((blocks, NBASE_DEV), 1)).astype(F32)
    count = jnp.sum(base_hot, axis=0, keepdims=True)
    r8 = iota((8, LANES), 0)
    for i in range(n_pix // 2):
        cols = slice(i * LANES, (i + 1) * LANES)
        for o, tile in zip((2 * i, 2 * i + 1), pair(where[0:8, cols], where[8:16, cols], swap_halves)):
            tile = jnp.where(r8 == 3, count, tile).astype(BF)
            for d in range(n_det):
                rest_ref[d * n_pix + o, half:, :] = tile


def join_kernel(mine_ref, took_ref, rest_ref, send_ref):
    rows, half, _ = mine_ref.shape
    for g in range(rows):
        send_ref[g, 0:half, :] = rest_ref[g, 0:half, :]
        send_ref[g, half : 2 * half, :] = (mine_ref[g] + took_ref[g].astype(F32)).astype(BF)
        send_ref[g, 2 * half :, :] = rest_ref[g, half:, :]


def split2(v):
    a = v.astype(BF)
    return a, (v - a.astype(F32)).astype(BF)


def total(v):
    return jnp.sum(jnp.sum(v, axis=0, keepdims=True), axis=1, keepdims=True)


def project(col_t, sky_t, pb_hot, base_hot, row_hot, shift=None):
    rows = row_hot.shape[0]
    spread = dot_nn(sky_t.astype(BF), pb_hot)
    spread = spread if shift is None else spread - shift
    per_slot = jnp.sum(col_t.astype(F32) * spread, axis=0, keepdims=True)
    parts = [jnp.where(row_hot, p.astype(F32), 0.0).astype(BF) for p in split2(per_slot)]
    both = dot_nt(jnp.concatenate(parts, axis=0), base_hot)
    return both[0:rows] + both[rows:]


def bin_amps(amps, col_t, pb_hot, base_hot, row_hot):
    rows = row_hot.shape[0]
    both = dot_nn(jnp.concatenate(split2(amps), axis=0), base_hot)
    per_slot = jnp.sum(jnp.where(row_hot, both[0:rows] + both[rows:], 0.0), axis=0, keepdims=True)
    return dot_nt((col_t.astype(F32) * per_slot).astype(BF), pb_hot)


def row_mask(rows, slots):
    return iota((rows, slots), 1) // CAP == iota((rows, slots), 0)


def halves_out(part, keep_ref, give_ref, work):
    work[...] = part
    half = keep_ref.shape[0]
    core = lax.rem(lax.axis_index("det"), 2)
    keep_ref[...] = work[pl.ds(pl.multiple_of(core * half, half), half), :]
    give_ref[...] = work[pl.ds(pl.multiple_of((1 - core) * half, half), half), :]


def sum_kernel(keep_ref, took_ref, send_ref):
    part = (keep_ref[...] + took_ref[...]).astype(BF)
    for g in range(send_ref.shape[0]):
        send_ref[g] = part


def total_of(got_ref, n_pix):
    sums = [None, None]
    for g in range(got_ref.shape[0]):
        core = (g // n_pix) % 2
        term = got_ref[g].astype(F32)
        sums[core] = term if sums[core] is None else sums[core] + term
    return jnp.concatenate(sums, axis=0)


def columns_of(pack_ref):
    slots = pack_ref.shape[1] - LANES
    inv = pack_ref[:, slots:].astype(F32)
    return pack_ref[:, :slots], inv[:, 0:PB_DEV] + inv[:, PB_DEV:]


def owner_kernel(pch, n_pix, got_ref, keep_ref, give_ref, pack_ref, pb_ref, hot_ref, more_ref, work, mean):
    rows = got_ref.shape[0]
    half = pch // 2
    slots = rows * CAP
    pb_of = iota((PB_DEV, LANES), 0).astype(F32)
    base_of = iota((NBASE_DEV, LANES), 0).astype(F32)
    maps = [jnp.zeros((half, LANES), F32), jnp.zeros((half, LANES), F32)]
    for g in range(rows):
        core = (g // n_pix) % 2
        maps[core] = maps[core] + got_ref[g, half : 2 * half, :].astype(F32)
    for i in range(rows // 2):
        cols = slice(i * LANES, (i + 1) * LANES)
        halves = pair(got_ref[2 * i, 0:half, :].astype(F32), got_ref[2 * i + 1, 0:half, :].astype(F32), swap_halves)
        pack_ref[0:half, cols] = halves[0].astype(BF)
        pack_ref[half:, cols] = halves[1].astype(BF)
        tiles = [got_ref[2 * i + k, 2 * half :, :].astype(F32) for k in (0, 1)]
        one, two = pair(*tiles, swap_halves)
        pb_ref[:, cols] = (pb_of == one[0:1]).astype(F32).astype(BF)
        hot_ref[:, cols] = (base_of == two[0:1]).astype(F32).astype(BF)
        mean[0:1, cols] = one[1:2] + two[1:2] + one[2:3]
        for k in (0, 1):
            more_ref[2 * i + k : 2 * i + k + 1, :] = tiles[k][3:4] + 1.0
    maps = jnp.concatenate(maps, axis=0)
    inv = 1.0 / (maps[:, 0:PB_DEV] + 1.0)
    pack_ref[:, slots:] = jnp.concatenate([v.astype(F32) for v in split2(inv)], axis=1).astype(BF)
    sky = maps[:, PB_DEV:] * inv
    part = project(pack_ref[:, :slots], sky, pb_ref[...], hot_ref[...], row_mask(rows, slots), mean[0:1, :])
    halves_out(part, keep_ref, give_ref, work)


def first_kernel(samples, n_pix, got_ref, pack_ref, other_ref, pb_ref, hot_ref, send_ref, rhs_ref, map_ref):
    rhs = total_of(got_ref, n_pix) * (-1.0 / samples)
    rhs_ref[...] = rhs
    rows = rhs.shape[0]
    slots = rows * CAP
    columns, inv = zip(columns_of(pack_ref), columns_of(other_ref))
    binned = bin_amps(rhs, jnp.concatenate(columns, axis=0), pb_ref[...], hot_ref[...], row_mask(rows, slots))
    map_ref[...] = binned[: pack_ref.shape[0]]
    sky = binned * jnp.concatenate(inv, axis=0)
    core = lax.rem(lax.axis_index("det"), 2)
    mine = pl.ds(pl.multiple_of(core * (slots // 2), slots // 2), slots // 2)
    columns = jnp.concatenate([pack_ref[:, mine], other_ref[:, mine]], axis=0)
    part = project(columns, sky, pb_ref[:, mine], hot_ref[:, mine], row_mask(rows // 2, slots // 2)).astype(BF)
    for g in range(rows):
        send_ref[g] = part


def second_kernel(samples, n_pix, got_ref, pack_ref, pb_ref, hot_ref, rhs_ref, map_ref, more_ref, send_ref, state_ref):
    rhs = rhs_ref[...]
    more = more_ref[...]
    image = more * rhs - total_of(got_ref, n_pix) * (1.0 / samples)
    rows = rhs.shape[0]
    columns, inv = columns_of(pack_ref)
    row_hot = row_mask(rows, columns.shape[1])
    image_map = bin_amps(image, columns, pb_ref[...], hot_ref[...], row_hot)
    rr = total(rhs * rhs)
    alpha = rr / total(rhs * image)
    error = rhs - alpha * image
    new = total(error * error)
    beta = new / rr
    heading = error + beta * rhs
    binned = (1.0 + beta) * map_ref[...] - alpha * image_map
    sky = binned * inv
    part = project(columns, sky, pb_ref[...], hot_ref[...], row_hot)
    quad = jnp.broadcast_to(total(binned * sky), (1, LANES))
    for g in range(rows):
        send_ref[g, 0:1, 0:LANES] = part[g : g + 1]
        send_ref[g, 0:1, LANES:] = quad
    scaled = more * heading
    state_ref[0] = alpha * rhs
    state_ref[1] = error
    state_ref[2] = heading
    state_ref[3] = scaled
    state_ref[4] = jnp.broadcast_to(new, (rows, LANES))
    state_ref[5] = jnp.broadcast_to(total(scaled * heading), (rows, LANES))


def last_kernel(samples, n_pix, got_ref, state_ref, levels_ref, error_ref):
    me = lax.axis_index("det") * n_pix + lax.axis_index("pix")
    acc = got_ref[0]
    for g in range(1, got_ref.shape[0]):
        acc = acc + got_ref[g]
    acc = acc * (1.0 / samples)
    mine = [state_ref[k, pl.ds(me, 1), :] for k in range(6)]
    levels, error, heading, scaled, new, curve = mine
    image = scaled - acc[:, 0:LANES]
    alpha = new / (curve - acc[:, LANES:])
    levels_ref[...] = levels + alpha * heading
    error_ref[...] = error - alpha * image


def call(kernel, outs, *args, scratch=()):
    vmem = pl.BlockSpec(memory_space=pltpu.VMEM)
    return pl.pallas_call(
        kernel,
        out_shape=outs,
        in_specs=[vmem] * len(args),
        out_specs=[vmem] * len(outs),
        scratch_shapes=scratch,
        compiler_params=pltpu.CompilerParams(vmem_limit_bytes=VMEM_LIMIT),
        cost_estimate=pl.CostEstimate(flops=10**8, bytes_accessed=4 * 10**6, transcendentals=0),
    )(*args)


def exchange(x):
    return lax.all_to_all(x, AXES, split_axis=0, concat_axis=0, tiled=True)


def other_core(x):
    return lax.ppermute(x, "det", [(i, i ^ 1) for i in range(lax.axis_size("det"))])


def body(timestream, weights, block_owner, block_local, baseline_of):
    n_det, n_pix = lax.axis_size("det"), lax.axis_size("pix")
    rows = n_det * n_pix
    _, blocks, samples, pixels = weights.shape
    pch = pixels // n_det
    half = pch // 2
    slots = rows * CAP
    group = 32
    shape = jax.ShapeDtypeStruct
    hbm = functools.partial(pltpu.with_memory_space_constraint, memory_space=pltpu.HBM)
    owners = block_owner.reshape(1, blocks)
    give, *filling = pl.pallas_call(
        functools.partial(bin_kernel, n_det, n_pix, group),
        out_shape=[
            shape((rows, half, LANES), BF),
            *[shape((pixels, blocks), F32)] * 3,
            shape((blocks, n_pix * PB_DEV), BF),
        ],
        in_specs=[pl.BlockSpec(memory_space=pltpu.HBM)] * 4,
        out_specs=[pl.BlockSpec(memory_space=pltpu.VMEM)] * 5,
        scratch_shapes=[
            pltpu.VMEM((blocks, samples, pixels), BF),
            pltpu.VMEM((1, blocks, samples), F32),
            *[pltpu.VMEM((1, blocks), jnp.int32)] * 2,
            *[pltpu.VMEM((blocks, pixels), F32)] * 3,
            pltpu.SemaphoreType.DMA((blocks // group + 1,)),
            pltpu.SemaphoreType.DMA((blocks // group + 3,)),
        ],
        compiler_params=pltpu.CompilerParams(vmem_limit_bytes=VMEM_LIMIT),
        cost_estimate=pl.CostEstimate(flops=10**8, bytes_accessed=2**25, transcendentals=0),
    )(hbm(timestream), weights, hbm(owners), hbm(block_local))
    took = other_core(give)
    mine, rest = call(
        functools.partial(fill_kernel, n_det, n_pix),
        [shape((rows, half, LANES), F32), shape((rows, half + 8, LANES), BF)],
        timestream, owners, block_local, baseline_of, *filling,
    )
    got = exchange(call(join_kernel, [shape((rows, pch + 8, LANES), BF)], mine, took, rest)[0])
    vector = shape((rows, NBASE_DEV), F32)
    part = shape((rows // 2, NBASE_DEV), F32)

    everyone = shape((rows, rows // 2, NBASE_DEV), BF)
    keep, give, pack, pb_hot, base_hot, more = call(
        functools.partial(owner_kernel, pch, n_pix),
        [part, part, shape((pch, slots + LANES), BF), shape((PB_DEV, slots), BF), shape((NBASE_DEV, slots), BF), vector],
        got,
        scratch=[pltpu.VMEM((rows, NBASE_DEV), F32), pltpu.VMEM((8, slots), F32)],
    )
    took, pack = lax.optimization_barrier((other_core(give), pack))
    other = other_core(pack)
    sent = call(sum_kernel, [everyone], keep, took)[0]
    sent, rhs, rhs_map = call(
        functools.partial(first_kernel, samples, n_pix), [everyone, vector, shape((pch, PB_DEV), F32)], exchange(sent), pack, other, pb_hot, base_hot
    )
    sent, state = call(
        functools.partial(second_kernel, samples, n_pix),
        [shape((rows, 1, 2 * LANES), F32), shape((6, rows, NBASE_DEV), F32)],
        exchange(sent), pack, pb_hot, base_hot, rhs, rhs_map, more,
    )
    own = shape((1, NBASE_DEV), F32)
    return tuple(call(functools.partial(last_kernel, samples, n_pix), [own, own], exchange(sent), state))


def solution(mesh):
    placed = (
        P(AXES, None, None),
        P(AXES, None, None, None),
        P(AXES, None, None),
        P(AXES, None),
        P(AXES, None),
    )
    return jax.shard_map(
        body,
        mesh=mesh,
        in_specs=placed,
        out_specs=(P(AXES, None), P(AXES, None)),
        check_vma=False,
    )
```

```python
import functools

import jax
import jax.numpy as jnp
from jax import lax
from jax.experimental import pallas as pl
from jax.experimental.pallas import tpu as pltpu
from jax.sharding import PartitionSpec as P

PB_DEV = 64
NBASE_DEV = 128
CAP = 64
LANES = 128
AXES = ("det", "pix")
BF = jnp.bfloat16
F32 = jnp.float32
VMEM_LIMIT = 48 * 1024 * 1024


def dot_nn(a, b):
    return lax.dot_general(a, b, (((1,), (0,)), ((), ())), preferred_element_type=F32)


def dot_nt(a, b):
    return lax.dot_general(a, b, (((1,), (1,)), ((), ())), preferred_element_type=F32)


def split3(v):
    a = v.astype(BF)
    left = v - a.astype(F32)
    b = left.astype(BF)
    c = (left - b.astype(F32)).astype(BF)
    return a, b, c


def iota(shape, dim):
    return lax.broadcasted_iota(jnp.int32, shape, dim)


def column(row):
    n = row.shape[1]
    eye = (iota((n, n), 0) == iota((n, n), 1)).astype(F32).astype(BF)
    return dot_nt(eye, jnp.broadcast_to(row.astype(F32).astype(BF), (8, n)))[:, 0:1].astype(jnp.int32)


def hot(target, wide):
    return (iota((target.shape[0], wide), 1) == target).astype(F32).astype(BF)


def bin_kernel(
    n_det, n_pix, group, ts_hbm, w_hbm, own_hbm, loc_hbm,
    give_ref, hit_ref, dat_ref, col_ref, pb_hot,
    w_s, ts_s, own_s, loc_s, hit_s, dat_s, sem, small,
):
    blocks, samples, pixels = ts_s.shape[0], ts_s.shape[1], w_s.shape[2]
    steps = blocks // group - 1
    short = group // 2

    def copies(first, many, k):
        where, pairs = pl.ds(2 * first, 2 * many), pl.ds(first, many)
        return (
            pltpu.make_async_copy(ts_hbm.at[0, where], ts_s.at[where], small.at[k]),
            pltpu.make_async_copy(w_hbm.at[pairs], w_s.at[pairs], sem.at[k]),
        )

    def full(c):
        return copies(c * short, short, c)

    ends = [copies(steps * short + k * short // 2, short // 2, steps + k) for k in (0, 1)]

    indices = [
        pltpu.make_async_copy(src, dst, small.at[steps + 2 + k]) for k, (src, dst) in enumerate(((own_hbm, own_s), (loc_hbm, loc_s)))
    ]
    for copy in indices:
        copy.start()
    for piece in [full(c) for c in range(steps)] + ends:
        for copy in piece:
            copy.start()
    place = iota((samples, LANES), 1)
    ones = jnp.ones((pixels, LANES), BF)
    row = iota((8, 2 * samples), 0) - jnp.where(iota((8, 2 * samples), 1) < samples, 0, 3)

    def row_sums(first, many):
        acc = jnp.zeros((samples, LANES), F32)
        for j in range(2 * many):
            w = w_s[first + j // 2, (j % 2) * samples : (j % 2 + 1) * samples, :]
            if j % 4 == 3:
                sums = dot_nn(w, ones)
            else:
                w = w.astype(F32)
                halves = w[:, 0:LANES]
                for k in range(LANES, pixels, LANES):
                    halves = halves + w[:, k : k + LANES]
                sums = jnp.sum(halves, axis=1, keepdims=True)
            acc = jnp.where(place == j, sums, acc)
        return acc.T[0 : 2 * many]

    def beside(one, two):
        return jnp.concatenate([jnp.broadcast_to(v, (8, samples)) for v in (one, two)], axis=1)

    def terms(first, many, sums):
        for j in range(many):
            r = beside(sums[2 * j : 2 * j + 1], sums[2 * j + 1 : 2 * j + 2])
            at = 2 * (first + j)
            u = beside(ts_s[pl.ds(at, 1), :], ts_s[pl.ds(at + 1, 1), :])
            lhs = jnp.where(row == 0, r, jnp.where(row == 1, u, jnp.where(row == 2, 1.0, 0.0))).astype(BF)
            t = dot_nn(lhs, w_s[first + j])
            for k in (0, 1):
                where = pl.ds(at + k, 1)
                hit_s[where, :] = t[3 * k : 3 * k + 1]
                dat_s[where, :] = t[3 * k + 1 : 3 * k + 2]
                col_ref[where, :] = t[3 * k + 2 : 3 * k + 3]

    def wait(piece):
        for copy in piece:
            copy.wait()

    def step(c, sums):
        wait(full(c))
        after = row_sums(c * short, short)
        terms((c - 1) * short, short, sums)
        return after

    wait(full(0))
    sums = lax.fori_loop(1, steps, step, row_sums(0, short))
    begin, quarter = steps * short, short // 2
    wait(ends[0])
    after = row_sums(begin, quarter)
    terms(begin - short, short, sums)
    wait(ends[1])
    last = row_sums(begin + quarter, quarter)
    terms(begin, quarter, after)
    for copy in indices:
        copy.wait()
    pb_hot[...] = hot(column(own_s[...]) * PB_DEV + column(loc_s[...]), n_pix * PB_DEV)
    terms(begin + quarter, quarter, last)
    hit_ref[...] = hit_s[...].T
    dat_ref[...] = dat_s[...].T
    core = lax.rem(lax.axis_index("det"), 2)
    binned(n_det, n_pix, 1 - core, hit_ref, dat_ref, pb_hot, give_ref)


def pair(first, second, swap):
    low = iota(first.shape, 1) < CAP
    return jnp.where(low, first, swap(second)), jnp.where(low, swap(first), second)


def swap_halves(v):
    return pltpu.roll(v, CAP, 1)


def two_up(n_det, n_pix, first, second, ref):
    half = first.shape[0] // n_det
    for i in range(n_pix // 2):
        cols = slice(i * LANES, (i + 1) * LANES)
        for o, tile in zip((2 * i, 2 * i + 1), pair(first[:, cols], second[:, cols], swap_halves)):
            tile = tile.astype(ref.dtype)
            for d in range(n_det):
                ref[d * n_pix + o, 0:half, :] = tile[d * half : (d + 1) * half]


def binned(n_det, n_pix, which, hit_ref, dat_ref, pb_hot, ref):
    half = hit_ref.shape[0] // n_det // 2
    rows = [
        of[pl.ds(pl.multiple_of((2 * d + which) * half, half), half), :].astype(BF) for of in (hit_ref, dat_ref) for d in range(n_det)
    ]
    both = dot_nn(jnp.concatenate(rows, axis=0), pb_hot[...])
    two_up(n_det, n_pix, both[: n_det * half], both[n_det * half :], ref)


def fill_kernel(n_det, n_pix, ts_ref, own_ref, loc_ref, base_ref, hit_ref, dat_ref, col_ref, pb_hot, mine_ref, rest_ref):
    _, blocks, samples = ts_ref.shape
    own = column(own_ref[...])
    tri = (iota((blocks, blocks), 1) < iota((blocks, blocks), 0)).astype(F32).astype(BF)
    own_hot = (own == iota((blocks, LANES), 1)).astype(F32)
    before = dot_nn(tri, own_hot.astype(BF))
    slot = own * CAP + jnp.sum(before * own_hot, axis=1, keepdims=True).astype(jnp.int32)
    slot_hot = hot(slot, n_pix * CAP)
    core = lax.rem(lax.axis_index("det"), 2)
    binned(n_det, n_pix, core, hit_ref, dat_ref, pb_hot, mine_ref)
    col_t = col_ref[...].T.astype(BF)
    pch = col_t.shape[0] // n_det
    half = pch // 2
    rows = [col_t[(2 * d + k) * half : (2 * d + k + 1) * half] for k in (0, 1) for d in range(n_det)]
    both = dot_nn(jnp.concatenate(rows, axis=0), slot_hot)
    two_up(n_det, n_pix, both[: n_det * half], both[n_det * half :], rest_ref)

    sums = jnp.sum(ts_ref[0].T, axis=0, keepdims=True)
    w0, w1, w2 = [w.astype(F32) for w in split3(sums / jnp.sum(col_t.astype(F32), axis=0, keepdims=True))]
    r16 = iota((16, blocks), 0)
    lhs = jnp.where(r16 == 0, loc_ref[...].astype(F32), jnp.where(r16 == 8, base_ref[...].astype(F32), 0.0))
    lhs = jnp.where(r16 == 1, w0, jnp.where(r16 == 9, w1, jnp.where(r16 == 2, w2, lhs)))
    where = dot_nn(lhs.astype(BF), slot_hot)
    base_hot = (column(base_ref[...]) == iota((blocks, NBASE_DEV), 1)).astype(F32)
    count = jnp.sum(base_hot, axis=0, keepdims=True)
    r8 = iota((8, LANES), 0)
    for i in range(n_pix // 2):
        cols = slice(i * LANES, (i + 1) * LANES)
        for o, tile in zip((2 * i, 2 * i + 1), pair(where[0:8, cols], where[8:16, cols], swap_halves)):
            tile = jnp.where(r8 == 3, count, tile).astype(BF)
            for d in range(n_det):
                rest_ref[d * n_pix + o, half:, :] = tile


def join_kernel(mine_ref, took_ref, rest_ref, send_ref):
    rows, half, _ = mine_ref.shape
    for g in range(rows):
        send_ref[g, 0:half, :] = rest_ref[g, 0:half, :]
        send_ref[g, half : 2 * half, :] = (mine_ref[g] + took_ref[g].astype(F32)).astype(BF)
        send_ref[g, 2 * half :, :] = rest_ref[g, half:, :]


def split2(v):
    a = v.astype(BF)
    return a, (v - a.astype(F32)).astype(BF)


def total(v):
    return jnp.sum(jnp.sum(v, axis=0, keepdims=True), axis=1, keepdims=True)


def project(col_t, sky_t, pb_hot, base_hot, row_hot, shift=None):
    rows = row_hot.shape[0]
    spread = dot_nn(sky_t.astype(BF), pb_hot)
    spread = spread if shift is None else spread - shift
    per_slot = jnp.sum(col_t.astype(F32) * spread, axis=0, keepdims=True)
    parts = [jnp.where(row_hot, p.astype(F32), 0.0).astype(BF) for p in split2(per_slot)]
    both = dot_nt(jnp.concatenate(parts, axis=0), base_hot)
    return both[0:rows] + both[rows:]


def bin_amps(amps, col_t, pb_hot, base_hot, row_hot):
    rows = row_hot.shape[0]
    both = dot_nn(jnp.concatenate(split2(amps), axis=0), base_hot)
    per_slot = jnp.sum(jnp.where(row_hot, both[0:rows] + both[rows:], 0.0), axis=0, keepdims=True)
    return dot_nt((col_t.astype(F32) * per_slot).astype(BF), pb_hot)


def row_mask(rows, slots):
    return iota((rows, slots), 1) // CAP == iota((rows, slots), 0)


def halves_out(part, keep_ref, give_ref, work):
    work[...] = part
    half = keep_ref.shape[0]
    core = lax.rem(lax.axis_index("det"), 2)
    keep_ref[...] = work[pl.ds(pl.multiple_of(core * half, half), half), :]
    give_ref[...] = work[pl.ds(pl.multiple_of((1 - core) * half, half), half), :]


def sum_kernel(keep_ref, took_ref, send_ref):
    part = (keep_ref[...] + took_ref[...]).astype(BF)
    for g in range(send_ref.shape[0]):
        send_ref[g] = part


def total_of(got_ref, n_pix):
    sums = [None, None]
    for g in range(got_ref.shape[0]):
        core = (g // n_pix) % 2
        term = got_ref[g].astype(F32)
        sums[core] = term if sums[core] is None else sums[core] + term
    return jnp.concatenate(sums, axis=0)


def columns_of(pack_ref):
    slots = pack_ref.shape[1] - LANES
    inv = pack_ref[:, slots:].astype(F32)
    return pack_ref[:, :slots], inv[:, 0:PB_DEV] + inv[:, PB_DEV:]


def owner_kernel(pch, n_pix, got_ref, keep_ref, give_ref, pack_ref, pb_ref, hot_ref, more_ref, work, mean):
    rows = got_ref.shape[0]
    half = pch // 2
    slots = rows * CAP
    pb_of = iota((PB_DEV, LANES), 0).astype(F32).astype(BF)
    base_of = iota((NBASE_DEV, LANES), 0).astype(F32).astype(BF)
    yes, no = jnp.ones((1, LANES), BF), jnp.zeros((1, LANES), BF)
    maps = [jnp.zeros((half, LANES), F32), jnp.zeros((half, LANES), F32)]
    for g in range(rows):
        core = (g // n_pix) % 2
        maps[core] = maps[core] + got_ref[g, half : 2 * half, :].astype(F32)
    for i in range(rows // 2):
        cols = slice(i * LANES, (i + 1) * LANES)
        halves = pair(got_ref[2 * i, 0:half, :].astype(F32), got_ref[2 * i + 1, 0:half, :].astype(F32), swap_halves)
        pack_ref[0:half, cols] = halves[0].astype(BF)
        pack_ref[half:, cols] = halves[1].astype(BF)
        tiles = [got_ref[2 * i + k, 2 * half :, :].astype(F32) for k in (0, 1)]
        one, two = pair(*tiles, swap_halves)
        pb_ref[:, cols] = jnp.where(pb_of == one[0:1].astype(BF), yes, no)
        hot_ref[:, cols] = jnp.where(base_of == two[0:1].astype(BF), yes, no)
        mean[0:1, cols] = one[1:2] + two[1:2] + one[2:3]
        for k in (0, 1):
            more_ref[2 * i + k : 2 * i + k + 1, :] = tiles[k][3:4] + 1.0
    maps = jnp.concatenate(maps, axis=0)
    inv = 1.0 / (maps[:, 0:PB_DEV] + 1.0)
    pack_ref[:, slots:] = jnp.concatenate([v.astype(F32) for v in split2(inv)], axis=1).astype(BF)
    sky = maps[:, PB_DEV:] * inv
    part = project(pack_ref[:, :slots], sky, pb_ref[...], hot_ref[...], row_mask(rows, slots), mean[0:1, :])
    halves_out(part, keep_ref, give_ref, work)


def first_kernel(samples, n_pix, got_ref, pack_ref, other_ref, pb_ref, hot_ref, send_ref, rhs_ref, map_ref):
    rhs = total_of(got_ref, n_pix) * (-1.0 / samples)
    rhs_ref[...] = rhs
    rows = rhs.shape[0]
    slots = rows * CAP
    columns, inv = zip(columns_of(pack_ref), columns_of(other_ref))
    binned = bin_amps(rhs, jnp.concatenate(columns, axis=0), pb_ref[...], hot_ref[...], row_mask(rows, slots))
    map_ref[...] = binned[: pack_ref.shape[0]]
    sky = binned * jnp.concatenate(inv, axis=0)
    core = lax.rem(lax.axis_index("det"), 2)
    mine = pl.ds(pl.multiple_of(core * (slots // 2), slots // 2), slots // 2)
    columns = jnp.concatenate([pack_ref[:, mine], other_ref[:, mine]], axis=0)
    part = project(columns, sky, pb_ref[:, mine], hot_ref[:, mine], row_mask(rows // 2, slots // 2)).astype(BF)
    for g in range(rows):
        send_ref[g] = part


def second_kernel(samples, n_pix, got_ref, pack_ref, pb_ref, hot_ref, rhs_ref, map_ref, more_ref, send_ref, state_ref):
    rhs = rhs_ref[...]
    more = more_ref[...]
    image = more * rhs - total_of(got_ref, n_pix) * (1.0 / samples)
    rows = rhs.shape[0]
    columns, inv = columns_of(pack_ref)
    row_hot = row_mask(rows, columns.shape[1])
    image_map = bin_amps(image, columns, pb_ref[...], hot_ref[...], row_hot)
    rr = total(rhs * rhs)
    alpha = rr / total(rhs * image)
    error = rhs - alpha * image
    new = total(error * error)
    beta = new / rr
    heading = error + beta * rhs
    binned = (1.0 + beta) * map_ref[...] - alpha * image_map
    sky = binned * inv
    part = project(columns, sky, pb_ref[...], hot_ref[...], row_hot)
    quad = jnp.broadcast_to(total(binned * sky), (1, LANES))
    for g in range(rows):
        send_ref[g, 0:1, 0:LANES] = part[g : g + 1]
        send_ref[g, 0:1, LANES:] = quad
    scaled = more * heading
    state_ref[0] = alpha * rhs
    state_ref[1] = error
    state_ref[2] = heading
    state_ref[3] = scaled
    state_ref[4] = jnp.broadcast_to(new, (rows, LANES))
    state_ref[5] = jnp.broadcast_to(total(scaled * heading), (rows, LANES))


def last_kernel(samples, n_pix, got_ref, state_ref, levels_ref, error_ref):
    me = lax.axis_index("det") * n_pix + lax.axis_index("pix")
    acc = got_ref[0]
    for g in range(1, got_ref.shape[0]):
        acc = acc + got_ref[g]
    acc = acc * (1.0 / samples)
    mine = [state_ref[k, pl.ds(me, 1), :] for k in range(6)]
    levels, error, heading, scaled, new, curve = mine
    image = scaled - acc[:, 0:LANES]
    alpha = new / (curve - acc[:, LANES:])
    levels_ref[...] = levels + alpha * heading
    error_ref[...] = error - alpha * image


def call(kernel, outs, *args, scratch=()):
    vmem = pl.BlockSpec(memory_space=pltpu.VMEM)
    return pl.pallas_call(
        kernel,
        out_shape=outs,
        in_specs=[vmem] * len(args),
        out_specs=[vmem] * len(outs),
        scratch_shapes=scratch,
        compiler_params=pltpu.CompilerParams(vmem_limit_bytes=VMEM_LIMIT),
        cost_estimate=pl.CostEstimate(flops=10**8, bytes_accessed=4 * 10**6, transcendentals=0),
    )(*args)


def exchange(x):
    return lax.all_to_all(x, AXES, split_axis=0, concat_axis=0, tiled=True)


def other_core(x):
    return lax.ppermute(x, "det", [(i, i ^ 1) for i in range(lax.axis_size("det"))])


def body(timestream, weights, block_owner, block_local, baseline_of):
    n_det, n_pix = lax.axis_size("det"), lax.axis_size("pix")
    rows = n_det * n_pix
    _, blocks, samples, pixels = weights.shape
    pch = pixels // n_det
    half = pch // 2
    slots = rows * CAP
    group = 32
    shape = jax.ShapeDtypeStruct
    hbm = functools.partial(pltpu.with_memory_space_constraint, memory_space=pltpu.HBM)
    owners = block_owner.reshape(1, blocks)
    give, *filling = pl.pallas_call(
        functools.partial(bin_kernel, n_det, n_pix, group),
        out_shape=[
            shape((rows, half, LANES), BF),
            *[shape((pixels, blocks), F32)] * 2,
            shape((blocks, pixels), F32),
            shape((blocks, n_pix * PB_DEV), BF),
        ],
        in_specs=[pl.BlockSpec(memory_space=pltpu.HBM)] * 4,
        out_specs=[pl.BlockSpec(memory_space=pltpu.VMEM)] * 5,
        scratch_shapes=[
            pltpu.VMEM((blocks // 2, 2 * samples, pixels), BF),
            pltpu.VMEM((blocks, samples), F32),
            *[pltpu.VMEM((1, blocks), jnp.int32)] * 2,
            *[pltpu.VMEM((blocks, pixels), F32)] * 2,
            pltpu.SemaphoreType.DMA((blocks // group + 1,)),
            pltpu.SemaphoreType.DMA((blocks // group + 3,)),
        ],
        compiler_params=pltpu.CompilerParams(vmem_limit_bytes=VMEM_LIMIT),
        cost_estimate=pl.CostEstimate(flops=10**8, bytes_accessed=2**25, transcendentals=0),
    )(hbm(timestream), weights.reshape(blocks // 2, 2 * samples, pixels), hbm(owners), hbm(block_local))
    took = other_core(give)
    mine, rest = call(
        functools.partial(fill_kernel, n_det, n_pix),
        [shape((rows, half, LANES), F32), shape((rows, half + 8, LANES), BF)],
        timestream, owners, block_local, baseline_of, *filling,
    )
    got = exchange(call(join_kernel, [shape((rows, pch + 8, LANES), BF)], mine, took, rest)[0])
    vector = shape((rows, NBASE_DEV), F32)
    part = shape((rows // 2, NBASE_DEV), F32)

    everyone = shape((rows, rows // 2, NBASE_DEV), BF)
    keep, give, pack, pb_hot, base_hot, more = call(
        functools.partial(owner_kernel, pch, n_pix),
        [part, part, shape((pch, slots + LANES), BF), shape((PB_DEV, slots), BF), shape((NBASE_DEV, slots), BF), vector],
        got,
        scratch=[pltpu.VMEM((rows, NBASE_DEV), F32), pltpu.VMEM((8, slots), F32)],
    )
    took, pack = lax.optimization_barrier((other_core(give), pack))
    other = other_core(pack)
    sent = call(sum_kernel, [everyone], keep, took)[0]
    sent, rhs, rhs_map = call(
        functools.partial(first_kernel, samples, n_pix), [everyone, vector, shape((pch, PB_DEV), F32)], exchange(sent), pack, other, pb_hot, base_hot
    )
    sent, state = call(
        functools.partial(second_kernel, samples, n_pix),
        [shape((rows, 1, 2 * LANES), F32), shape((6, rows, NBASE_DEV), F32)],
        exchange(sent), pack, pb_hot, base_hot, rhs, rhs_map, more,
    )
    own = shape((1, NBASE_DEV), F32)
    return tuple(call(functools.partial(last_kernel, samples, n_pix), [own, own], exchange(sent), state))


def solution(mesh):
    placed = (
        P(AXES, None, None),
        P(AXES, None, None, None),
        P(AXES, None, None),
        P(AXES, None),
        P(AXES, None),
    )
    return jax.shard_map(
        body,
        mesh=mesh,
        in_specs=placed,
        out_specs=(P(AXES, None), P(AXES, None)),
        check_vma=False,
    )
```

```python
import functools

import jax
import jax.numpy as jnp
from jax import lax
from jax.experimental import pallas as pl
from jax.experimental.pallas import tpu as pltpu
from jax.sharding import PartitionSpec as P

PB_DEV = 64
NBASE_DEV = 128
CAP = 64
LANES = 128
AXES = ("det", "pix")
BF = jnp.bfloat16
F32 = jnp.float32
VMEM_LIMIT = 48 * 1024 * 1024


def dot_nn(a, b):
    return lax.dot_general(a, b, (((1,), (0,)), ((), ())), preferred_element_type=F32)


def dot_nt(a, b):
    return lax.dot_general(a, b, (((1,), (1,)), ((), ())), preferred_element_type=F32)


def split3(v):
    a = v.astype(BF)
    left = v - a.astype(F32)
    b = left.astype(BF)
    c = (left - b.astype(F32)).astype(BF)
    return a, b, c


def iota(shape, dim):
    return lax.broadcasted_iota(jnp.int32, shape, dim)


def column(row):
    n = row.shape[1]
    eye = (iota((n, n), 0) == iota((n, n), 1)).astype(F32).astype(BF)
    return dot_nt(eye, jnp.broadcast_to(row.astype(F32).astype(BF), (8, n)))[:, 0:1].astype(jnp.int32)


def hot(target, wide):
    return (iota((target.shape[0], wide), 1) == target).astype(F32).astype(BF)


def bin_kernel(
    n_det, n_pix, group, ts_hbm, w_hbm, own_hbm, loc_hbm,
    give_ref, hit_ref, dat_ref, col_ref, pb_hot,
    w_s, ts_s, own_s, loc_s, hit_s, dat_s, sem, small,
):
    blocks, samples, pixels = ts_s.shape[0], ts_s.shape[1], w_s.shape[2]
    steps = blocks // group - 1
    short = group // 2

    def copies(first, many, k):
        where, pairs = pl.ds(2 * first, 2 * many), pl.ds(first, many)
        return (
            pltpu.make_async_copy(ts_hbm.at[0, where], ts_s.at[where], small.at[k]),
            pltpu.make_async_copy(w_hbm.at[pairs], w_s.at[pairs], sem.at[k]),
        )

    def full(c):
        return copies(c * short, short, c)

    ends = [copies(steps * short + k * short // 2, short // 2, steps + k) for k in (0, 1)]

    indices = [
        pltpu.make_async_copy(src, dst, small.at[steps + 2 + k]) for k, (src, dst) in enumerate(((own_hbm, own_s), (loc_hbm, loc_s)))
    ]
    for copy in indices:
        copy.start()
    for piece in [full(c) for c in range(steps)] + ends:
        for copy in piece:
            copy.start()
    place = iota((samples, LANES), 1)
    ones = jnp.ones((pixels, LANES), BF)
    row = iota((8, 2 * samples), 0) - jnp.where(iota((8, 2 * samples), 1) < samples, 0, 3)

    def row_sums(first, many):
        acc = jnp.zeros((samples, LANES), F32)
        for j in range(2 * many):
            w = w_s[first + j // 2, (j % 2) * samples : (j % 2 + 1) * samples, :]
            if j % 4 == 3:
                sums = dot_nn(w, ones)
            else:
                w = w.astype(F32)
                halves = w[:, 0:LANES]
                for k in range(LANES, pixels, LANES):
                    halves = halves + w[:, k : k + LANES]
                sums = jnp.sum(halves, axis=1, keepdims=True)
            acc = jnp.where(place == j, sums, acc)
        return acc.T[0 : 2 * many]

    def beside(one, two):
        return jnp.concatenate([jnp.broadcast_to(v, (8, samples)) for v in (one, two)], axis=1)

    def terms(first, many, sums):
        for j in range(many):
            r = beside(sums[2 * j : 2 * j + 1], sums[2 * j + 1 : 2 * j + 2])
            at = 2 * (first + j)
            u = beside(ts_s[pl.ds(at, 1), :], ts_s[pl.ds(at + 1, 1), :])
            lhs = jnp.where(row == 0, r, jnp.where(row == 1, u, jnp.where(row == 2, 1.0, 0.0))).astype(BF)
            t = dot_nn(lhs, w_s[first + j])
            for k in (0, 1):
                where = pl.ds(at + k, 1)
                hit_s[where, :] = t[3 * k : 3 * k + 1]
                dat_s[where, :] = t[3 * k + 1 : 3 * k + 2]
                col_ref[where, :] = t[3 * k + 2 : 3 * k + 3]

    def wait(piece):
        for copy in piece:
            copy.wait()

    def step(c, sums):
        wait(full(c))
        after = row_sums(c * short, short)
        terms((c - 1) * short, short, sums)
        return after

    wait(full(0))
    sums = lax.fori_loop(1, steps, step, row_sums(0, short))
    begin, quarter = steps * short, short // 2
    wait(ends[0])
    after = row_sums(begin, quarter)
    terms(begin - short, short, sums)
    wait(ends[1])
    last = row_sums(begin + quarter, quarter)
    terms(begin, quarter, after)
    for copy in indices:
        copy.wait()
    pb_hot[...] = hot(column(own_s[...]) * PB_DEV + column(loc_s[...]), n_pix * PB_DEV)
    terms(begin + quarter, quarter, last)
    hit_ref[...] = hit_s[...].T
    dat_ref[...] = dat_s[...].T
    core = lax.rem(lax.axis_index("det"), 2)
    binned(n_det, n_pix, 1 - core, hit_ref, dat_ref, pb_hot, give_ref)


def pair(first, second, swap):
    low = iota(first.shape, 1) < CAP
    return jnp.where(low, first, swap(second)), jnp.where(low, swap(first), second)


def swap_halves(v):
    return pltpu.roll(v, CAP, 1)


def two_up(n_det, n_pix, first, second, ref):
    half = first.shape[0] // n_det
    for i in range(n_pix // 2):
        cols = slice(i * LANES, (i + 1) * LANES)
        for o, tile in zip((2 * i, 2 * i + 1), pair(first[:, cols], second[:, cols], swap_halves)):
            tile = tile.astype(ref.dtype)
            for d in range(n_det):
                ref[d * n_pix + o, 0:half, :] = tile[d * half : (d + 1) * half]


def binned(n_det, n_pix, which, hit_ref, dat_ref, pb_hot, ref):
    half = hit_ref.shape[0] // n_det // 2
    rows = [
        of[pl.ds(pl.multiple_of((2 * d + which) * half, half), half), :].astype(BF) for of in (hit_ref, dat_ref) for d in range(n_det)
    ]
    both = dot_nn(jnp.concatenate(rows, axis=0), pb_hot[...])
    two_up(n_det, n_pix, both[: n_det * half], both[n_det * half :], ref)


def fill_kernel(n_det, n_pix, ts_ref, own_ref, loc_ref, base_ref, hit_ref, dat_ref, col_ref, pb_hot, mine_ref, rest_ref):
    _, blocks, samples = ts_ref.shape
    own = column(own_ref[...])
    tri = (iota((blocks, blocks), 1) < iota((blocks, blocks), 0)).astype(F32).astype(BF)
    own_hot = (own == iota((blocks, LANES), 1)).astype(F32)
    before = dot_nn(tri, own_hot.astype(BF))
    slot = own * CAP + jnp.sum(before * own_hot, axis=1, keepdims=True).astype(jnp.int32)
    slot_hot = hot(slot, n_pix * CAP)
    core = lax.rem(lax.axis_index("det"), 2)
    binned(n_det, n_pix, core, hit_ref, dat_ref, pb_hot, mine_ref)
    col_t = col_ref[...].T.astype(BF)
    pch = col_t.shape[0] // n_det
    half = pch // 2
    rows = [col_t[(2 * d + k) * half : (2 * d + k + 1) * half] for k in (0, 1) for d in range(n_det)]
    both = dot_nn(jnp.concatenate(rows, axis=0), slot_hot)
    two_up(n_det, n_pix, both[: n_det * half], both[n_det * half :], rest_ref)

    sums = jnp.sum(ts_ref[0].T, axis=0, keepdims=True)
    w0, w1, w2 = [w.astype(F32) for w in split3(sums / jnp.sum(col_t.astype(F32), axis=0, keepdims=True))]
    r16 = iota((16, blocks), 0)
    lhs = jnp.where(r16 == 0, loc_ref[...].astype(F32), jnp.where(r16 == 8, base_ref[...].astype(F32), 0.0))
    lhs = jnp.where(r16 == 1, w0, jnp.where(r16 == 9, w1, jnp.where(r16 == 2, w2, lhs)))
    where = dot_nn(lhs.astype(BF), slot_hot)
    base_hot = (column(base_ref[...]) == iota((blocks, NBASE_DEV), 1)).astype(F32)
    count = jnp.sum(base_hot, axis=0, keepdims=True)
    r8 = iota((8, LANES), 0)
    for i in range(n_pix // 2):
        cols = slice(i * LANES, (i + 1) * LANES)
        for o, tile in zip((2 * i, 2 * i + 1), pair(where[0:8, cols], where[8:16, cols], swap_halves)):
            tile = jnp.where(r8 == 3, count, tile).astype(BF)
            for d in range(n_det):
                rest_ref[d * n_pix + o, half:, :] = tile


def join_kernel(mine_ref, took_ref, rest_ref, send_ref):
    rows, half, _ = mine_ref.shape
    for g in range(rows):
        send_ref[g, 0:half, :] = rest_ref[g, 0:half, :]
        send_ref[g, half : 2 * half, :] = (mine_ref[g] + took_ref[g].astype(F32)).astype(BF)
        send_ref[g, 2 * half :, :] = rest_ref[g, half:, :]


def split2(v):
    a = v.astype(BF)
    return a, (v - a.astype(F32)).astype(BF)


def total(v):
    return jnp.sum(jnp.sum(v, axis=0, keepdims=True), axis=1, keepdims=True)


def project(col_t, sky_t, pb_hot, collapse, row_hot, shift=None):
    rows = row_hot.shape[0]
    spread = dot_nn(sky_t.astype(BF), pb_hot)
    spread = spread if shift is None else spread - shift
    per_slot = jnp.sum(col_t.astype(F32) * spread, axis=0, keepdims=True)
    parts = [jnp.where(row_hot, p.astype(F32), 0.0).astype(BF) for p in split2(per_slot)]
    both = collapse(jnp.concatenate(parts, axis=0))
    return both[0:rows] + both[rows:]


def bin_amps(amps, col_t, pb_back, base_hot, row_hot):
    rows = row_hot.shape[0]
    both = dot_nn(jnp.concatenate(split2(amps), axis=0), base_hot)
    per_slot = jnp.sum(jnp.where(row_hot, both[0:rows] + both[rows:], 0.0), axis=0, keepdims=True)
    return dot_nn((col_t.astype(F32) * per_slot).astype(BF), pb_back)


def row_mask(rows, slots):
    return iota((rows, slots), 1) // CAP == iota((rows, slots), 0)


def halves_out(part, keep_ref, give_ref, work):
    work[...] = part
    half = keep_ref.shape[0]
    core = lax.rem(lax.axis_index("det"), 2)
    keep_ref[...] = work[pl.ds(pl.multiple_of(core * half, half), half), :]
    give_ref[...] = work[pl.ds(pl.multiple_of((1 - core) * half, half), half), :]


def sum_kernel(keep_ref, took_ref, send_ref):
    part = (keep_ref[...] + took_ref[...]).astype(BF)
    for g in range(send_ref.shape[0]):
        send_ref[g] = part


def total_of(got_ref, n_pix):
    sums = [None, None]
    for g in range(got_ref.shape[0]):
        core = (g // n_pix) % 2
        term = got_ref[g].astype(F32)
        sums[core] = term if sums[core] is None else sums[core] + term
    return jnp.concatenate(sums, axis=0)


def columns_of(pack_ref):
    slots = pack_ref.shape[1] - LANES
    inv = pack_ref[:, slots:].astype(F32)
    return pack_ref[:, :slots], inv[:, 0:PB_DEV] + inv[:, PB_DEV:]


def owner_kernel(pch, n_pix, got_ref, keep_ref, give_ref, pack_ref, pb_ref, hot_ref, more_ref, work, mean):
    rows = got_ref.shape[0]
    half = pch // 2
    slots = rows * CAP
    pb_of = iota((PB_DEV, LANES), 0).astype(F32).astype(BF)
    base_of = iota((NBASE_DEV, LANES), 0).astype(F32).astype(BF)
    yes, no = jnp.ones((1, LANES), BF), jnp.zeros((1, LANES), BF)
    maps = [jnp.zeros((half, LANES), F32), jnp.zeros((half, LANES), F32)]
    for g in range(rows):
        core = (g // n_pix) % 2
        maps[core] = maps[core] + got_ref[g, half : 2 * half, :].astype(F32)
    for i in range(rows // 2):
        cols = slice(i * LANES, (i + 1) * LANES)
        halves = pair(got_ref[2 * i, 0:half, :].astype(F32), got_ref[2 * i + 1, 0:half, :].astype(F32), swap_halves)
        pack_ref[0:half, cols] = halves[0].astype(BF)
        pack_ref[half:, cols] = halves[1].astype(BF)
        tiles = [got_ref[2 * i + k, 2 * half :, :].astype(F32) for k in (0, 1)]
        one, two = pair(*tiles, swap_halves)
        pb_ref[:, cols] = jnp.where(pb_of == one[0:1].astype(BF), yes, no)
        hot_ref[:, cols] = jnp.where(base_of == two[0:1].astype(BF), yes, no)
        mean[0:1, cols] = one[1:2] + two[1:2] + one[2:3]
        for k in (0, 1):
            more_ref[2 * i + k : 2 * i + k + 1, :] = tiles[k][3:4] + 1.0
    maps = jnp.concatenate(maps, axis=0)
    inv = 1.0 / (maps[:, 0:PB_DEV] + 1.0)
    pack_ref[:, slots:] = jnp.concatenate([v.astype(F32) for v in split2(inv)], axis=1).astype(BF)
    sky = maps[:, PB_DEV:] * inv
    collapse = lambda v: dot_nt(v, hot_ref[...])
    part = project(pack_ref[:, :slots], sky, pb_ref[...], collapse, row_mask(rows, slots), mean[0:1, :])
    halves_out(part, keep_ref, give_ref, work)


def turn_kernel(pb_ref, hot_ref, pb_back_ref, hot_back_ref):
    for k in range(0, pb_ref.shape[1], LANES):
        for ref, back in ((pb_ref, pb_back_ref), (hot_ref, hot_back_ref)):
            back[k : k + LANES, :] = ref[:, k : k + LANES].astype(F32).T.astype(BF)


def first_kernel(samples, n_pix, got_ref, pack_ref, other_ref, pb_ref, hot_ref, pb_back, hot_back, send_ref, rhs_ref, map_ref):
    rhs = total_of(got_ref, n_pix) * (-1.0 / samples)
    rhs_ref[...] = rhs
    rows = rhs.shape[0]
    slots = rows * CAP
    columns, inv = zip(columns_of(pack_ref), columns_of(other_ref))
    binned = bin_amps(rhs, jnp.concatenate(columns, axis=0), pb_back[...], hot_ref[...], row_mask(rows, slots))
    map_ref[...] = binned[: pack_ref.shape[0]]
    sky = binned * jnp.concatenate(inv, axis=0)
    core = lax.rem(lax.axis_index("det"), 2)
    mine = pl.ds(pl.multiple_of(core * (slots // 2), slots // 2), slots // 2)
    columns = jnp.concatenate([pack_ref[:, mine], other_ref[:, mine]], axis=0)
    collapse = lambda v: dot_nn(v, hot_back[mine, :])
    part = project(columns, sky, pb_ref[:, mine], collapse, row_mask(rows // 2, slots // 2)).astype(BF)
    for g in range(rows):
        send_ref[g] = part


def second_kernel(
    samples, n_pix, got_ref, pack_ref, pb_ref, hot_ref, pb_back, hot_back, rhs_ref, map_ref, more_ref, send_ref, state_ref
):
    rhs = rhs_ref[...]
    more = more_ref[...]
    image = more * rhs - total_of(got_ref, n_pix) * (1.0 / samples)
    rows = rhs.shape[0]
    columns, inv = columns_of(pack_ref)
    row_hot = row_mask(rows, columns.shape[1])
    image_map = bin_amps(image, columns, pb_back[...], hot_ref[...], row_hot)
    rr = total(rhs * rhs)
    alpha = rr / total(rhs * image)
    error = rhs - alpha * image
    new = total(error * error)
    beta = new / rr
    heading = error + beta * rhs
    binned = (1.0 + beta) * map_ref[...] - alpha * image_map
    sky = binned * inv
    part = project(columns, sky, pb_ref[...], lambda v: dot_nn(v, hot_back[...]), row_hot)
    quad = jnp.broadcast_to(total(binned * sky), (1, LANES))
    for g in range(rows):
        send_ref[g, 0:1, 0:LANES] = part[g : g + 1]
        send_ref[g, 0:1, LANES:] = quad
    scaled = more * heading
    state_ref[0] = alpha * rhs
    state_ref[1] = error
    state_ref[2] = heading
    state_ref[3] = scaled
    state_ref[4] = jnp.broadcast_to(new, (rows, LANES))
    state_ref[5] = jnp.broadcast_to(total(scaled * heading), (rows, LANES))


def last_kernel(samples, n_pix, got_ref, state_ref, levels_ref, error_ref):
    me = lax.axis_index("det") * n_pix + lax.axis_index("pix")
    acc = got_ref[0]
    for g in range(1, got_ref.shape[0]):
        acc = acc + got_ref[g]
    acc = acc * (1.0 / samples)
    mine = [state_ref[k, pl.ds(me, 1), :] for k in range(6)]
    levels, error, heading, scaled, new, curve = mine
    image = scaled - acc[:, 0:LANES]
    alpha = new / (curve - acc[:, LANES:])
    levels_ref[...] = levels + alpha * heading
    error_ref[...] = error - alpha * image


def call(kernel, outs, *args, scratch=()):
    vmem = pl.BlockSpec(memory_space=pltpu.VMEM)
    return pl.pallas_call(
        kernel,
        out_shape=outs,
        in_specs=[vmem] * len(args),
        out_specs=[vmem] * len(outs),
        scratch_shapes=scratch,
        compiler_params=pltpu.CompilerParams(vmem_limit_bytes=VMEM_LIMIT),
        cost_estimate=pl.CostEstimate(flops=10**8, bytes_accessed=4 * 10**6, transcendentals=0),
    )(*args)


def exchange(x):
    return lax.all_to_all(x, AXES, split_axis=0, concat_axis=0, tiled=True)


def other_core(x):
    return lax.ppermute(x, "det", [(i, i ^ 1) for i in range(lax.axis_size("det"))])


def body(timestream, weights, block_owner, block_local, baseline_of):
    n_det, n_pix = lax.axis_size("det"), lax.axis_size("pix")
    rows = n_det * n_pix
    _, blocks, samples, pixels = weights.shape
    pch = pixels // n_det
    half = pch // 2
    slots = rows * CAP
    group = 32
    shape = jax.ShapeDtypeStruct
    hbm = functools.partial(pltpu.with_memory_space_constraint, memory_space=pltpu.HBM)
    owners = block_owner.reshape(1, blocks)
    give, *filling = pl.pallas_call(
        functools.partial(bin_kernel, n_det, n_pix, group),
        out_shape=[
            shape((rows, half, LANES), BF),
            *[shape((pixels, blocks), F32)] * 2,
            shape((blocks, pixels), F32),
            shape((blocks, n_pix * PB_DEV), BF),
        ],
        in_specs=[pl.BlockSpec(memory_space=pltpu.HBM)] * 4,
        out_specs=[pl.BlockSpec(memory_space=pltpu.VMEM)] * 5,
        scratch_shapes=[
            pltpu.VMEM((blocks // 2, 2 * samples, pixels), BF),
            pltpu.VMEM((blocks, samples), F32),
            *[pltpu.VMEM((1, blocks), jnp.int32)] * 2,
            *[pltpu.VMEM((blocks, pixels), F32)] * 2,
            pltpu.SemaphoreType.DMA((blocks // group + 1,)),
            pltpu.SemaphoreType.DMA((blocks // group + 3,)),
        ],
        compiler_params=pltpu.CompilerParams(vmem_limit_bytes=VMEM_LIMIT),
        cost_estimate=pl.CostEstimate(flops=10**8, bytes_accessed=2**25, transcendentals=0),
    )(hbm(timestream), weights.reshape(blocks // 2, 2 * samples, pixels), hbm(owners), hbm(block_local))
    took = other_core(give)
    mine, rest = call(
        functools.partial(fill_kernel, n_det, n_pix),
        [shape((rows, half, LANES), F32), shape((rows, half + 8, LANES), BF)],
        timestream, owners, block_local, baseline_of, *filling,
    )
    got = exchange(call(join_kernel, [shape((rows, pch + 8, LANES), BF)], mine, took, rest)[0])
    vector = shape((rows, NBASE_DEV), F32)
    part = shape((rows // 2, NBASE_DEV), F32)

    everyone = shape((rows, rows // 2, NBASE_DEV), BF)
    keep, give, pack, pb_hot, base_hot, more = call(
        functools.partial(owner_kernel, pch, n_pix),
        [part, part, shape((pch, slots + LANES), BF), shape((PB_DEV, slots), BF), shape((NBASE_DEV, slots), BF), vector],
        got,
        scratch=[pltpu.VMEM((rows, NBASE_DEV), F32), pltpu.VMEM((8, slots), F32)],
    )
    backs = call(turn_kernel, [shape((slots, PB_DEV), BF), shape((slots, NBASE_DEV), BF)], pb_hot, base_hot)
    took, pack, *backs = lax.optimization_barrier((other_core(give), pack, *backs))
    other = other_core(pack)
    sent = call(sum_kernel, [everyone], keep, took)[0]
    sent, rhs, rhs_map = call(
        functools.partial(first_kernel, samples, n_pix), [everyone, vector, shape((pch, PB_DEV), F32)], exchange(sent), pack, other, pb_hot, base_hot, *backs
    )
    sent, state = call(
        functools.partial(second_kernel, samples, n_pix),
        [shape((rows, 1, 2 * LANES), F32), shape((6, rows, NBASE_DEV), F32)],
        exchange(sent), pack, pb_hot, base_hot, *backs, rhs, rhs_map, more,
    )
    own = shape((1, NBASE_DEV), F32)
    return tuple(call(functools.partial(last_kernel, samples, n_pix), [own, own], exchange(sent), state))


def solution(mesh):
    placed = (
        P(AXES, None, None),
        P(AXES, None, None, None),
        P(AXES, None, None),
        P(AXES, None),
        P(AXES, None),
    )
    return jax.shard_map(
        body,
        mesh=mesh,
        in_specs=placed,
        out_specs=(P(AXES, None), P(AXES, None)),
        check_vma=False,
    )
```

```python
import functools

import jax
import jax.numpy as jnp
from jax import lax
from jax.experimental import pallas as pl
from jax.experimental.pallas import tpu as pltpu
from jax.sharding import PartitionSpec as P

PB_DEV = 64
NBASE_DEV = 128
CAP = 64
LANES = 128
AXES = ("det", "pix")
BF = jnp.bfloat16
F32 = jnp.float32
VMEM_LIMIT = 48 * 1024 * 1024


def dot_nn(a, b):
    return lax.dot_general(a, b, (((1,), (0,)), ((), ())), preferred_element_type=F32)


def dot_nt(a, b):
    return lax.dot_general(a, b, (((1,), (1,)), ((), ())), preferred_element_type=F32)


def split3(v):
    a = v.astype(BF)
    left = v - a.astype(F32)
    b = left.astype(BF)
    c = (left - b.astype(F32)).astype(BF)
    return a, b, c


def iota(shape, dim):
    return lax.broadcasted_iota(jnp.int32, shape, dim)


def column(row):
    n = row.shape[1]
    eye = (iota((n, n), 0) == iota((n, n), 1)).astype(F32).astype(BF)
    return dot_nt(eye, jnp.broadcast_to(row.astype(F32).astype(BF), (8, n)))[:, 0:1].astype(jnp.int32)


def hot(target, wide):
    return (iota((target.shape[0], wide), 1) == target).astype(F32).astype(BF)


def bin_kernel(
    n_det, n_pix, group, ts_hbm, w_hbm, own_hbm, loc_hbm,
    give_ref, hit_ref, dat_ref, col_ref, pb_hot,
    w_s, ts_s, own_s, loc_s, hit_s, dat_s, sem, small,
):
    blocks, samples, pixels = ts_s.shape[0], ts_s.shape[1], w_s.shape[2]
    steps = blocks // group - 1
    short = group // 2

    def copies(first, many, k):
        where, pairs = pl.ds(2 * first, 2 * many), pl.ds(first, many)
        return (
            pltpu.make_async_copy(ts_hbm.at[0, where], ts_s.at[where], small.at[k]),
            pltpu.make_async_copy(w_hbm.at[pairs], w_s.at[pairs], sem.at[k]),
        )

    def full(c):
        return copies(c * short, short, c)

    ends = [copies(steps * short + k * short // 2, short // 2, steps + k) for k in (0, 1)]

    indices = [
        pltpu.make_async_copy(src, dst, small.at[steps + 2 + k]) for k, (src, dst) in enumerate(((own_hbm, own_s), (loc_hbm, loc_s)))
    ]
    for copy in indices:
        copy.start()
    for piece in [full(c) for c in range(steps)] + ends:
        for copy in piece:
            copy.start()
    place = iota((samples, LANES), 1)
    ones = jnp.ones((pixels, LANES), BF)
    row = iota((8, 2 * samples), 0) - jnp.where(iota((8, 2 * samples), 1) < samples, 0, 3)

    def row_sums(first, many, every=4):
        acc = jnp.zeros((samples, LANES), F32)
        for j in range(2 * many):
            w = w_s[first + j // 2, (j % 2) * samples : (j % 2 + 1) * samples, :]
            if j % every == every - 1:
                sums = dot_nn(w, ones)
            else:
                w = w.astype(F32)
                halves = w[:, 0:LANES]
                for k in range(LANES, pixels, LANES):
                    halves = halves + w[:, k : k + LANES]
                sums = jnp.sum(halves, axis=1, keepdims=True)
            acc = jnp.where(place == j, sums, acc)
        return acc.T[0 : 2 * many]

    def beside(one, two):
        return jnp.concatenate([jnp.broadcast_to(v, (8, samples)) for v in (one, two)], axis=1)

    def terms(first, many, sums):
        for j in range(many):
            r = beside(sums[2 * j : 2 * j + 1], sums[2 * j + 1 : 2 * j + 2])
            at = 2 * (first + j)
            u = beside(ts_s[pl.ds(at, 1), :], ts_s[pl.ds(at + 1, 1), :])
            lhs = jnp.where(row == 0, r, jnp.where(row == 1, u, jnp.where(row == 2, 1.0, 0.0))).astype(BF)
            t = dot_nn(lhs, w_s[first + j])
            for k in (0, 1):
                where = pl.ds(at + k, 1)
                hit_s[where, :] = t[3 * k : 3 * k + 1]
                dat_s[where, :] = t[3 * k + 1 : 3 * k + 2]
                col_ref[where, :] = t[3 * k + 2 : 3 * k + 3]

    def wait(piece):
        for copy in piece:
            copy.wait()

    def step(c, sums):
        wait(full(c))
        after = row_sums(c * short, short)
        terms((c - 1) * short, short, sums)
        return after

    wait(full(0))
    sums = lax.fori_loop(1, steps, step, row_sums(0, short))
    begin, quarter = steps * short, short // 2
    wait(ends[0])
    after = row_sums(begin, quarter, 3)
    terms(begin - short, short, sums)
    wait(ends[1])
    last = row_sums(begin + quarter, quarter, 2)
    terms(begin, quarter, after)
    for copy in indices:
        copy.wait()
    pb_hot[...] = hot(column(own_s[...]) * PB_DEV + column(loc_s[...]), n_pix * PB_DEV)
    terms(begin + quarter, quarter, last)
    hit_ref[...] = hit_s[...].T
    dat_ref[...] = dat_s[...].T
    core = lax.rem(lax.axis_index("det"), 2)
    binned(n_det, n_pix, 1 - core, hit_ref, dat_ref, pb_hot, give_ref)


def pair(first, second, swap):
    low = iota(first.shape, 1) < CAP
    return jnp.where(low, first, swap(second)), jnp.where(low, swap(first), second)


def swap_halves(v):
    return pltpu.roll(v, CAP, 1)


def two_up(n_det, n_pix, first, second, ref):
    half = first.shape[0] // n_det
    for i in range(n_pix // 2):
        cols = slice(i * LANES, (i + 1) * LANES)
        for o, tile in zip((2 * i, 2 * i + 1), pair(first[:, cols], second[:, cols], swap_halves)):
            tile = tile.astype(ref.dtype)
            for d in range(n_det):
                ref[d * n_pix + o, 0:half, :] = tile[d * half : (d + 1) * half]


def binned(n_det, n_pix, which, hit_ref, dat_ref, pb_hot, ref):
    half = hit_ref.shape[0] // n_det // 2
    rows = [
        of[pl.ds(pl.multiple_of((2 * d + which) * half, half), half), :].astype(BF) for of in (hit_ref, dat_ref) for d in range(n_det)
    ]
    both = dot_nn(jnp.concatenate(rows, axis=0), pb_hot[...])
    two_up(n_det, n_pix, both[: n_det * half], both[n_det * half :], ref)


def fill_kernel(n_det, n_pix, ts_ref, own_ref, loc_ref, base_ref, hit_ref, dat_ref, col_ref, pb_hot, mine_ref, rest_ref):
    _, blocks, samples = ts_ref.shape
    own = column(own_ref[...])
    tri = (iota((blocks, blocks), 1) < iota((blocks, blocks), 0)).astype(F32).astype(BF)
    own_hot = (own == iota((blocks, LANES), 1)).astype(F32)
    before = dot_nn(tri, own_hot.astype(BF))
    slot = own * CAP + jnp.sum(before * own_hot, axis=1, keepdims=True).astype(jnp.int32)
    slot_hot = hot(slot, n_pix * CAP)
    core = lax.rem(lax.axis_index("det"), 2)
    binned(n_det, n_pix, core, hit_ref, dat_ref, pb_hot, mine_ref)
    col_t = col_ref[...].T.astype(BF)
    pch = col_t.shape[0] // n_det
    half = pch // 2
    rows = [col_t[(2 * d + k) * half : (2 * d + k + 1) * half] for k in (0, 1) for d in range(n_det)]
    both = dot_nn(jnp.concatenate(rows, axis=0), slot_hot)
    two_up(n_det, n_pix, both[: n_det * half], both[n_det * half :], rest_ref)

    sums = jnp.sum(ts_ref[0].T, axis=0, keepdims=True)
    w0, w1, w2 = [w.astype(F32) for w in split3(sums / jnp.sum(col_t.astype(F32), axis=0, keepdims=True))]
    r16 = iota((16, blocks), 0)
    lhs = jnp.where(r16 == 0, loc_ref[...].astype(F32), jnp.where(r16 == 8, base_ref[...].astype(F32), 0.0))
    lhs = jnp.where(r16 == 1, w0, jnp.where(r16 == 9, w1, jnp.where(r16 == 2, w2, lhs)))
    where = dot_nn(lhs.astype(BF), slot_hot)
    base_hot = (column(base_ref[...]) == iota((blocks, NBASE_DEV), 1)).astype(F32)
    count = jnp.sum(base_hot, axis=0, keepdims=True)
    r8 = iota((8, LANES), 0)
    for i in range(n_pix // 2):
        cols = slice(i * LANES, (i + 1) * LANES)
        for o, tile in zip((2 * i, 2 * i + 1), pair(where[0:8, cols], where[8:16, cols], swap_halves)):
            tile = jnp.where(r8 == 3, count, tile).astype(BF)
            for d in range(n_det):
                rest_ref[d * n_pix + o, half:, :] = tile


def join_kernel(mine_ref, took_ref, rest_ref, send_ref):
    rows, half, _ = mine_ref.shape
    for g in range(rows):
        send_ref[g, 0:half, :] = rest_ref[g, 0:half, :]
        send_ref[g, half : 2 * half, :] = (mine_ref[g] + took_ref[g].astype(F32)).astype(BF)
        send_ref[g, 2 * half :, :] = rest_ref[g, half:, :]


def split2(v):
    a = v.astype(BF)
    return a, (v - a.astype(F32)).astype(BF)


def total(v):
    return jnp.sum(jnp.sum(v, axis=0, keepdims=True), axis=1, keepdims=True)


def project(col_t, sky_t, pb_hot, collapse, row_hot, shift=None):
    rows = row_hot.shape[0]
    spread = dot_nn(sky_t.astype(BF), pb_hot)
    spread = spread if shift is None else spread - shift
    per_slot = jnp.sum(col_t.astype(F32) * spread, axis=0, keepdims=True)
    parts = [jnp.where(row_hot, p.astype(F32), 0.0).astype(BF) for p in split2(per_slot)]
    both = collapse(jnp.concatenate(parts, axis=0))
    return both[0:rows] + both[rows:]


def bin_amps(amps, col_t, pb_back, base_hot, row_hot):
    rows = row_hot.shape[0]
    both = dot_nn(jnp.concatenate(split2(amps), axis=0), base_hot)
    per_slot = jnp.sum(jnp.where(row_hot, both[0:rows] + both[rows:], 0.0), axis=0, keepdims=True)
    return dot_nn((col_t.astype(F32) * per_slot).astype(BF), pb_back)


def row_mask(rows, slots):
    return iota((rows, slots), 1) // CAP == iota((rows, slots), 0)


def halves_out(part, keep_ref, give_ref, work):
    work[...] = part
    half = keep_ref.shape[0]
    core = lax.rem(lax.axis_index("det"), 2)
    keep_ref[...] = work[pl.ds(pl.multiple_of(core * half, half), half), :]
    give_ref[...] = work[pl.ds(pl.multiple_of((1 - core) * half, half), half), :]


def sum_kernel(keep_ref, took_ref, send_ref):
    part = (keep_ref[...] + took_ref[...]).astype(BF)
    for g in range(send_ref.shape[0]):
        send_ref[g] = part


def total_of(got_ref, n_pix):
    sums = [None, None]
    for g in range(got_ref.shape[0]):
        core = (g // n_pix) % 2
        term = got_ref[g].astype(F32)
        sums[core] = term if sums[core] is None else sums[core] + term
    return jnp.concatenate(sums, axis=0)


def columns_of(pack_ref):
    slots = pack_ref.shape[1] - LANES
    inv = pack_ref[:, slots:].astype(F32)
    return pack_ref[:, :slots], inv[:, 0:PB_DEV] + inv[:, PB_DEV:]


def owner_kernel(pch, n_pix, got_ref, keep_ref, give_ref, col_ref, inv_ref, pb_ref, hot_ref, work, mean):
    rows = got_ref.shape[0]
    half = pch // 2
    slots = rows * CAP
    pb_of = iota((PB_DEV, LANES), 0).astype(F32).astype(BF)
    base_of = iota((NBASE_DEV, LANES), 0).astype(F32).astype(BF)
    yes, no = jnp.ones((1, LANES), BF), jnp.zeros((1, LANES), BF)
    maps = [jnp.zeros((half, LANES), F32), jnp.zeros((half, LANES), F32)]
    for g in range(rows):
        core = (g // n_pix) % 2
        maps[core] = maps[core] + got_ref[g, half : 2 * half, :].astype(F32)
    for i in range(rows // 2):
        cols = slice(i * LANES, (i + 1) * LANES)
        halves = pair(got_ref[2 * i, 0:half, :].astype(F32), got_ref[2 * i + 1, 0:half, :].astype(F32), swap_halves)
        col_ref[0:half, cols] = halves[0].astype(BF)
        col_ref[half:, cols] = halves[1].astype(BF)
        tiles = [got_ref[2 * i + k, 2 * half :, :].astype(F32) for k in (0, 1)]
        one, two = pair(*tiles, swap_halves)
        pb_ref[:, cols] = jnp.where(pb_of == one[0:1].astype(BF), yes, no)
        hot_ref[:, cols] = jnp.where(base_of == two[0:1].astype(BF), yes, no)
        mean[0:1, cols] = one[1:2] + two[1:2] + one[2:3]
    maps = jnp.concatenate(maps, axis=0)
    inv = 1.0 / (maps[:, 0:PB_DEV] + 1.0)
    inv_ref[...] = inv
    sky = maps[:, PB_DEV:] * inv
    collapse = lambda v: dot_nt(v, hot_ref[...])
    part = project(col_ref[...], sky, pb_ref[...], collapse, row_mask(rows, slots), mean[0:1, :])
    halves_out(part, keep_ref, give_ref, work)


def turn_kernel(got_ref, col_ref, inv_ref, pb_ref, hot_ref, pack_ref, pb_back_ref, hot_back_ref, more_ref):
    pch, slots = col_ref.shape
    pack_ref[:, :slots] = col_ref[...]
    pack_ref[:, slots:] = jnp.concatenate([v.astype(F32) for v in split2(inv_ref[...])], axis=1).astype(BF)
    for k in range(0, slots, LANES):
        for ref, back in ((pb_ref, pb_back_ref), (hot_ref, hot_back_ref)):
            back[k : k + LANES, :] = ref[:, k : k + LANES].astype(F32).T.astype(BF)
    for g in range(got_ref.shape[0]):
        more_ref[g : g + 1, :] = got_ref[g, pch:, :].astype(F32)[3:4] + 1.0


def first_kernel(samples, n_pix, got_ref, pack_ref, other_ref, pb_ref, hot_ref, pb_back, hot_back, send_ref, rhs_ref, map_ref):
    rhs = total_of(got_ref, n_pix) * (-1.0 / samples)
    rhs_ref[...] = rhs
    rows = rhs.shape[0]
    slots = rows * CAP
    columns, inv = zip(columns_of(pack_ref), columns_of(other_ref))
    binned = bin_amps(rhs, jnp.concatenate(columns, axis=0), pb_back[...], hot_ref[...], row_mask(rows, slots))
    map_ref[...] = binned[: pack_ref.shape[0]]
    sky = binned * jnp.concatenate(inv, axis=0)
    core = lax.rem(lax.axis_index("det"), 2)
    mine = pl.ds(pl.multiple_of(core * (slots // 2), slots // 2), slots // 2)
    columns = jnp.concatenate([pack_ref[:, mine], other_ref[:, mine]], axis=0)
    collapse = lambda v: dot_nn(v, hot_back[mine, :])
    part = project(columns, sky, pb_ref[:, mine], collapse, row_mask(rows // 2, slots // 2)).astype(BF)
    for g in range(rows):
        send_ref[g] = part


def second_kernel(
    samples, n_pix, got_ref, pack_ref, pb_ref, hot_ref, pb_back, hot_back, rhs_ref, map_ref, more_ref, send_ref, state_ref
):
    rhs = rhs_ref[...]
    more = more_ref[...]
    image = more * rhs - total_of(got_ref, n_pix) * (1.0 / samples)
    rows = rhs.shape[0]
    columns, inv = columns_of(pack_ref)
    row_hot = row_mask(rows, columns.shape[1])
    image_map = bin_amps(image, columns, pb_back[...], hot_ref[...], row_hot)
    rr = total(rhs * rhs)
    alpha = rr / total(rhs * image)
    error = rhs - alpha * image
    new = total(error * error)
    beta = new / rr
    heading = error + beta * rhs
    binned = (1.0 + beta) * map_ref[...] - alpha * image_map
    sky = binned * inv
    part = project(columns, sky, pb_ref[...], lambda v: dot_nn(v, hot_back[...]), row_hot)
    quad = jnp.broadcast_to(total(binned * sky), (1, LANES))
    for g in range(rows):
        send_ref[g, 0:1, 0:LANES] = part[g : g + 1]
        send_ref[g, 0:1, LANES:] = quad
    scaled = more * heading
    state_ref[0] = alpha * rhs
    state_ref[1] = error
    state_ref[2] = heading
    state_ref[3] = scaled
    state_ref[4] = jnp.broadcast_to(new, (rows, LANES))
    state_ref[5] = jnp.broadcast_to(total(scaled * heading), (rows, LANES))


def last_kernel(samples, n_pix, got_ref, state_ref, levels_ref, error_ref):
    me = lax.axis_index("det") * n_pix + lax.axis_index("pix")
    acc = got_ref[0]
    for g in range(1, got_ref.shape[0]):
        acc = acc + got_ref[g]
    acc = acc * (1.0 / samples)
    mine = [state_ref[k, pl.ds(me, 1), :] for k in range(6)]
    levels, error, heading, scaled, new, curve = mine
    image = scaled - acc[:, 0:LANES]
    alpha = new / (curve - acc[:, LANES:])
    levels_ref[...] = levels + alpha * heading
    error_ref[...] = error - alpha * image


def call(kernel, outs, *args, scratch=()):
    vmem = pl.BlockSpec(memory_space=pltpu.VMEM)
    return pl.pallas_call(
        kernel,
        out_shape=outs,
        in_specs=[vmem] * len(args),
        out_specs=[vmem] * len(outs),
        scratch_shapes=scratch,
        compiler_params=pltpu.CompilerParams(vmem_limit_bytes=VMEM_LIMIT),
        cost_estimate=pl.CostEstimate(flops=10**8, bytes_accessed=4 * 10**6, transcendentals=0),
    )(*args)


def exchange(x):
    return lax.all_to_all(x, AXES, split_axis=0, concat_axis=0, tiled=True)


def other_core(x):
    return lax.ppermute(x, "det", [(i, i ^ 1) for i in range(lax.axis_size("det"))])


def body(timestream, weights, block_owner, block_local, baseline_of):
    n_det, n_pix = lax.axis_size("det"), lax.axis_size("pix")
    rows = n_det * n_pix
    _, blocks, samples, pixels = weights.shape
    pch = pixels // n_det
    half = pch // 2
    slots = rows * CAP
    group = 32
    shape = jax.ShapeDtypeStruct
    hbm = functools.partial(pltpu.with_memory_space_constraint, memory_space=pltpu.HBM)
    owners = block_owner.reshape(1, blocks)
    give, *filling = pl.pallas_call(
        functools.partial(bin_kernel, n_det, n_pix, group),
        out_shape=[
            shape((rows, half, LANES), BF),
            *[shape((pixels, blocks), F32)] * 2,
            shape((blocks, pixels), F32),
            shape((blocks, n_pix * PB_DEV), BF),
        ],
        in_specs=[pl.BlockSpec(memory_space=pltpu.HBM)] * 4,
        out_specs=[pl.BlockSpec(memory_space=pltpu.VMEM)] * 5,
        scratch_shapes=[
            pltpu.VMEM((blocks // 2, 2 * samples, pixels), BF),
            pltpu.VMEM((blocks, samples), F32),
            *[pltpu.VMEM((1, blocks), jnp.int32)] * 2,
            *[pltpu.VMEM((blocks, pixels), F32)] * 2,
            pltpu.SemaphoreType.DMA((blocks // group + 1,)),
            pltpu.SemaphoreType.DMA((blocks // group + 3,)),
        ],
        compiler_params=pltpu.CompilerParams(vmem_limit_bytes=VMEM_LIMIT),
        cost_estimate=pl.CostEstimate(flops=10**8, bytes_accessed=2**25, transcendentals=0),
    )(hbm(timestream), weights.reshape(blocks // 2, 2 * samples, pixels), hbm(owners), hbm(block_local))
    took = other_core(give)
    mine, rest = call(
        functools.partial(fill_kernel, n_det, n_pix),
        [shape((rows, half, LANES), F32), shape((rows, half + 8, LANES), BF)],
        timestream, owners, block_local, baseline_of, *filling,
    )
    got = exchange(call(join_kernel, [shape((rows, pch + 8, LANES), BF)], mine, took, rest)[0])
    vector = shape((rows, NBASE_DEV), F32)
    part = shape((rows // 2, NBASE_DEV), F32)

    everyone = shape((rows, rows // 2, NBASE_DEV), BF)
    keep, give, col_t, inv, pb_hot, base_hot = call(
        functools.partial(owner_kernel, pch, n_pix),
        [
            part, part, shape((pch, slots), BF), shape((pch, PB_DEV), F32),
            shape((PB_DEV, slots), BF), shape((NBASE_DEV, slots), BF),
        ],
        got,
        scratch=[pltpu.VMEM((rows, NBASE_DEV), F32), pltpu.VMEM((8, slots), F32)],
    )
    turned = call(
        turn_kernel,
        [shape((pch, slots + LANES), BF), shape((slots, PB_DEV), BF), shape((slots, NBASE_DEV), BF), vector],
        got, col_t, inv, pb_hot, base_hot,
    )
    took, pack, *backs, more = lax.optimization_barrier((other_core(give), *turned))
    other = other_core(pack)
    sent = call(sum_kernel, [everyone], keep, took)[0]
    sent, rhs, rhs_map = call(
        functools.partial(first_kernel, samples, n_pix), [everyone, vector, shape((pch, PB_DEV), F32)], exchange(sent), pack, other, pb_hot, base_hot, *backs
    )
    sent, state = call(
        functools.partial(second_kernel, samples, n_pix),
        [shape((rows, 1, 2 * LANES), F32), shape((6, rows, NBASE_DEV), F32)],
        exchange(sent), pack, pb_hot, base_hot, *backs, rhs, rhs_map, more,
    )
    own = shape((1, NBASE_DEV), F32)
    return tuple(call(functools.partial(last_kernel, samples, n_pix), [own, own], exchange(sent), state))


def solution(mesh):
    placed = (
        P(AXES, None, None),
        P(AXES, None, None, None),
        P(AXES, None, None),
        P(AXES, None),
        P(AXES, None),
    )
    return jax.shard_map(
        body,
        mesh=mesh,
        in_specs=placed,
        out_specs=(P(AXES, None), P(AXES, None)),
        check_vma=False,
    )
```

```python
import functools

import jax
import jax.numpy as jnp
from jax import lax
from jax.experimental import pallas as pl
from jax.experimental.pallas import tpu as pltpu
from jax.sharding import PartitionSpec as P

PB_DEV = 64
NBASE_DEV = 128
CAP = 64
LANES = 128
AXES = ("det", "pix")
BF = jnp.bfloat16
F32 = jnp.float32
VMEM_LIMIT = 48 * 1024 * 1024


def dot_nn(a, b):
    return lax.dot_general(a, b, (((1,), (0,)), ((), ())), preferred_element_type=F32)


def dot_nt(a, b):
    return lax.dot_general(a, b, (((1,), (1,)), ((), ())), preferred_element_type=F32)


def split3(v):
    a = v.astype(BF)
    left = v - a.astype(F32)
    b = left.astype(BF)
    c = (left - b.astype(F32)).astype(BF)
    return a, b, c


def iota(shape, dim):
    return lax.broadcasted_iota(jnp.int32, shape, dim)


def column(row):
    n = row.shape[1]
    eye = (iota((n, n), 0) == iota((n, n), 1)).astype(F32).astype(BF)
    return dot_nt(eye, jnp.broadcast_to(row.astype(F32).astype(BF), (8, n)))[:, 0:1].astype(jnp.int32)


def hot(target, wide):
    return (iota((target.shape[0], wide), 1) == target).astype(F32).astype(BF)


def bin_kernel(
    n_det, n_pix, group, ts_hbm, w_hbm, own_hbm, loc_hbm,
    give_ref, hit_ref, dat_ref, col_ref, pb_hot,
    w_s, ts_s, own_s, loc_s, hit_s, dat_s, sem, small,
):
    blocks, samples, pixels = ts_s.shape[0], ts_s.shape[1], w_s.shape[2]
    steps = blocks // group - 1
    short = group // 2

    def copies(first, many, k):
        where, pairs = pl.ds(2 * first, 2 * many), pl.ds(first, many)
        return (
            pltpu.make_async_copy(ts_hbm.at[0, where], ts_s.at[where], small.at[k]),
            pltpu.make_async_copy(w_hbm.at[pairs], w_s.at[pairs], sem.at[k]),
        )

    def full(c):
        return copies(c * short, short, c)

    ends = [copies(steps * short + k * short // 2, short // 2, steps + k) for k in (0, 1)]

    indices = [
        pltpu.make_async_copy(src, dst, small.at[steps + 2 + k]) for k, (src, dst) in enumerate(((own_hbm, own_s), (loc_hbm, loc_s)))
    ]
    for copy in indices:
        copy.start()
    for piece in [full(c) for c in range(steps)] + ends:
        for copy in piece:
            copy.start()
    place = iota((samples, LANES), 1)
    ones = jnp.ones((pixels, LANES), BF)
    row = iota((8, 2 * samples), 0) - jnp.where(iota((8, 2 * samples), 1) < samples, 0, 3)

    def row_sums(first, many, every=4):
        acc = jnp.zeros((samples, LANES), F32)
        for j in range(2 * many):
            w = w_s[first + j // 2, (j % 2) * samples : (j % 2 + 1) * samples, :]
            if j % every == every - 1:
                sums = dot_nn(w, ones)
            else:
                w = w.astype(F32)
                halves = w[:, 0:LANES]
                for k in range(LANES, pixels, LANES):
                    halves = halves + w[:, k : k + LANES]
                sums = jnp.sum(halves, axis=1, keepdims=True)
            acc = jnp.where(place == j, sums, acc)
        return acc.T[0 : 2 * many]

    def beside(one, two):
        return jnp.concatenate([jnp.broadcast_to(v, (8, samples)) for v in (one, two)], axis=1)

    def terms(first, many, sums):
        for j in range(many):
            r = beside(sums[2 * j : 2 * j + 1], sums[2 * j + 1 : 2 * j + 2])
            at = 2 * (first + j)
            u = beside(ts_s[pl.ds(at, 1), :], ts_s[pl.ds(at + 1, 1), :])
            lhs = jnp.where(row == 0, r, jnp.where(row == 1, u, jnp.where(row == 2, 1.0, 0.0))).astype(BF)
            t = dot_nn(lhs, w_s[first + j])
            for k in (0, 1):
                where = pl.ds(at + k, 1)
                hit_s[where, :] = t[3 * k : 3 * k + 1]
                dat_s[where, :] = t[3 * k + 1 : 3 * k + 2]
                col_ref[where, :] = t[3 * k + 2 : 3 * k + 3]

    def wait(piece):
        for copy in piece:
            copy.wait()

    def step(c, sums):
        wait(full(c))
        after = row_sums(c * short, short)
        terms((c - 1) * short, short, sums)
        return after

    wait(full(0))
    sums = lax.fori_loop(1, steps, step, row_sums(0, short))
    begin, quarter = steps * short, short // 2
    wait(ends[0])
    after = row_sums(begin, quarter, 3)
    terms(begin - short, short, sums)
    wait(ends[1])
    last = row_sums(begin + quarter, quarter, 2)
    terms(begin, quarter, after)
    for copy in indices:
        copy.wait()
    pb_hot[...] = hot(column(own_s[...]) * PB_DEV + column(loc_s[...]), n_pix * PB_DEV)
    terms(begin + quarter, quarter, last)
    hit_ref[...] = hit_s[...].T
    dat_ref[...] = dat_s[...].T
    core = lax.rem(lax.axis_index("det"), 2)
    binned(n_det, n_pix, 1 - core, hit_ref, dat_ref, pb_hot, give_ref)


def pair(first, second, swap):
    low = iota(first.shape, 1) < CAP
    return jnp.where(low, first, swap(second)), jnp.where(low, swap(first), second)


def swap_halves(v):
    return pltpu.roll(v, CAP, 1)


def two_up(n_det, n_pix, first, second, ref):
    half = first.shape[0] // n_det
    for i in range(n_pix // 2):
        cols = slice(i * LANES, (i + 1) * LANES)
        for o, tile in zip((2 * i, 2 * i + 1), pair(first[:, cols], second[:, cols], swap_halves)):
            tile = tile.astype(ref.dtype)
            for d in range(n_det):
                ref[o * n_det + d, 0:half, :] = tile[d * half : (d + 1) * half]


def binned(n_det, n_pix, which, hit_ref, dat_ref, pb_hot, ref):
    half = hit_ref.shape[0] // n_det // 2
    rows = [
        of[pl.ds(pl.multiple_of((2 * d + which) * half, half), half), :].astype(BF) for of in (hit_ref, dat_ref) for d in range(n_det)
    ]
    both = dot_nn(jnp.concatenate(rows, axis=0), pb_hot[...])
    two_up(n_det, n_pix, both[: n_det * half], both[n_det * half :], ref)


def fill_kernel(n_det, n_pix, ts_ref, own_ref, loc_ref, base_ref, hit_ref, dat_ref, col_ref, pb_hot, mine_ref, rest_ref):
    _, blocks, samples = ts_ref.shape
    own = column(own_ref[...])
    tri = (iota((blocks, blocks), 1) < iota((blocks, blocks), 0)).astype(F32).astype(BF)
    own_hot = (own == iota((blocks, LANES), 1)).astype(F32)
    before = dot_nn(tri, own_hot.astype(BF))
    slot = own * CAP + jnp.sum(before * own_hot, axis=1, keepdims=True).astype(jnp.int32)
    slot_hot = hot(slot, n_pix * CAP)
    core = lax.rem(lax.axis_index("det"), 2)
    binned(n_det, n_pix, core, hit_ref, dat_ref, pb_hot, mine_ref)
    col_t = col_ref[...].T.astype(BF)
    pch = col_t.shape[0] // n_det
    half = pch // 2
    rows = [col_t[(2 * d + k) * half : (2 * d + k + 1) * half] for k in (0, 1) for d in range(n_det)]
    both = dot_nn(jnp.concatenate(rows, axis=0), slot_hot)
    two_up(n_det, n_pix, both[: n_det * half], both[n_det * half :], rest_ref)

    sums = jnp.sum(ts_ref[0].T, axis=0, keepdims=True)
    w0, w1, w2 = [w.astype(F32) for w in split3(sums / jnp.sum(col_t.astype(F32), axis=0, keepdims=True))]
    r16 = iota((16, blocks), 0)
    lhs = jnp.where(r16 == 0, loc_ref[...].astype(F32), jnp.where(r16 == 8, base_ref[...].astype(F32), 0.0))
    lhs = jnp.where(r16 == 1, w0, jnp.where(r16 == 9, w1, jnp.where(r16 == 2, w2, lhs)))
    where = dot_nn(lhs.astype(BF), slot_hot)
    base_hot = (column(base_ref[...]) == iota((blocks, NBASE_DEV), 1)).astype(F32)
    count = jnp.sum(base_hot, axis=0, keepdims=True)
    r8 = iota((8, LANES), 0)
    for i in range(n_pix // 2):
        cols = slice(i * LANES, (i + 1) * LANES)
        for o, tile in zip((2 * i, 2 * i + 1), pair(where[0:8, cols], where[8:16, cols], swap_halves)):
            tile = jnp.where(r8 == 3, count, tile).astype(BF)
            for d in range(n_det):
                rest_ref[o * n_det + d, half:, :] = tile


def join_kernel(mine_ref, took_ref, rest_ref, send_ref):
    rows, half, _ = mine_ref.shape
    for g in range(rows):
        send_ref[g, 0:half, :] = rest_ref[g, 0:half, :]
        send_ref[g, half : 2 * half, :] = (mine_ref[g] + took_ref[g].astype(F32)).astype(BF)
        send_ref[g, 2 * half :, :] = rest_ref[g, half:, :]


def split2(v):
    a = v.astype(BF)
    return a, (v - a.astype(F32)).astype(BF)


def total(v):
    return jnp.sum(jnp.sum(v, axis=0, keepdims=True), axis=1, keepdims=True)


def project(col_t, sky_t, pb_hot, collapse, row_hot, shift=None):
    rows = row_hot.shape[0]
    spread = dot_nn(sky_t.astype(BF), pb_hot)
    spread = spread if shift is None else spread - shift
    per_slot = jnp.sum(col_t.astype(F32) * spread, axis=0, keepdims=True)
    parts = [jnp.where(row_hot, p.astype(F32), 0.0).astype(BF) for p in split2(per_slot)]
    both = collapse(jnp.concatenate(parts, axis=0))
    return both[0:rows] + both[rows:]


def bin_amps(amps, col_t, pb_back, base_hot, row_hot):
    rows = row_hot.shape[0]
    both = dot_nn(jnp.concatenate(split2(amps), axis=0), base_hot)
    per_slot = jnp.sum(jnp.where(row_hot, both[0:rows] + both[rows:], 0.0), axis=0, keepdims=True)
    return dot_nn((col_t.astype(F32) * per_slot).astype(BF), pb_back)


def row_mask(rows, slots):
    return iota((rows, slots), 1) // CAP == iota((rows, slots), 0)


def halves_out(part, keep_ref, give_ref, work):
    work[...] = part
    half = keep_ref.shape[0]
    core = lax.rem(lax.axis_index("det"), 2)
    keep_ref[...] = work[pl.ds(pl.multiple_of(core * half, half), half), :]
    give_ref[...] = work[pl.ds(pl.multiple_of((1 - core) * half, half), half), :]


def sum_kernel(keep_ref, took_ref, send_ref):
    part = (keep_ref[...] + took_ref[...]).astype(BF)
    for g in range(send_ref.shape[0]):
        send_ref[g] = part


def total_of(got_ref):
    sums = [None, None]
    for g in range(got_ref.shape[0]):
        core = g % 2
        term = got_ref[g].astype(F32)
        sums[core] = term if sums[core] is None else sums[core] + term
    return jnp.concatenate(sums, axis=0)


def columns_of(pack_ref):
    slots = pack_ref.shape[1] - LANES
    inv = pack_ref[:, slots:].astype(F32)
    return pack_ref[:, :slots], inv[:, 0:PB_DEV] + inv[:, PB_DEV:]


def owner_kernel(pch, got_ref, keep_ref, give_ref, col_ref, inv_ref, pb_ref, hot_ref, work, mean):
    rows = got_ref.shape[0]
    half = pch // 2
    slots = rows * CAP
    pb_of = iota((PB_DEV, LANES), 0).astype(F32).astype(BF)
    base_of = iota((NBASE_DEV, LANES), 0).astype(F32).astype(BF)
    yes, no = jnp.ones((1, LANES), BF), jnp.zeros((1, LANES), BF)
    maps = [jnp.zeros((half, LANES), F32), jnp.zeros((half, LANES), F32)]
    for g in range(rows):
        core = g % 2
        maps[core] = maps[core] + got_ref[g, half : 2 * half, :].astype(F32)
    for i in range(rows // 2):
        cols = slice(i * LANES, (i + 1) * LANES)
        halves = pair(got_ref[2 * i, 0:half, :].astype(F32), got_ref[2 * i + 1, 0:half, :].astype(F32), swap_halves)
        col_ref[0:half, cols] = halves[0].astype(BF)
        col_ref[half:, cols] = halves[1].astype(BF)
        tiles = [got_ref[2 * i + k, 2 * half :, :].astype(F32) for k in (0, 1)]
        one, two = pair(*tiles, swap_halves)
        pb_ref[:, cols] = jnp.where(pb_of == one[0:1].astype(BF), yes, no)
        hot_ref[:, cols] = jnp.where(base_of == two[0:1].astype(BF), yes, no)
        mean[0:1, cols] = one[1:2] + two[1:2] + one[2:3]
    maps = jnp.concatenate(maps, axis=0)
    inv = 1.0 / (maps[:, 0:PB_DEV] + 1.0)
    inv_ref[...] = inv
    sky = maps[:, PB_DEV:] * inv
    collapse = lambda v: dot_nt(v, hot_ref[...])
    part = project(col_ref[...], sky, pb_ref[...], collapse, row_mask(rows, slots), mean[0:1, :])
    halves_out(part, keep_ref, give_ref, work)


def turn_kernel(got_ref, col_ref, inv_ref, pb_ref, hot_ref, pack_ref, pb_back_ref, hot_back_ref, more_ref):
    pch, slots = col_ref.shape
    pack_ref[:, :slots] = col_ref[...]
    pack_ref[:, slots:] = jnp.concatenate([v.astype(F32) for v in split2(inv_ref[...])], axis=1).astype(BF)
    for k in range(0, slots, LANES):
        for ref, back in ((pb_ref, pb_back_ref), (hot_ref, hot_back_ref)):
            back[k : k + LANES, :] = ref[:, k : k + LANES].astype(F32).T.astype(BF)
    for g in range(got_ref.shape[0]):
        more_ref[g : g + 1, :] = got_ref[g, pch:, :].astype(F32)[3:4] + 1.0


def first_kernel(samples, got_ref, pack_ref, other_ref, pb_ref, hot_ref, pb_back, hot_back, send_ref, rhs_ref, map_ref):
    rhs = total_of(got_ref) * (-1.0 / samples)
    rhs_ref[...] = rhs
    rows = rhs.shape[0]
    slots = rows * CAP
    columns, inv = zip(columns_of(pack_ref), columns_of(other_ref))
    binned = bin_amps(rhs, jnp.concatenate(columns, axis=0), pb_back[...], hot_ref[...], row_mask(rows, slots))
    map_ref[...] = binned[: pack_ref.shape[0]]
    sky = binned * jnp.concatenate(inv, axis=0)
    core = lax.rem(lax.axis_index("det"), 2)
    mine = pl.ds(pl.multiple_of(core * (slots // 2), slots // 2), slots // 2)
    columns = jnp.concatenate([pack_ref[:, mine], other_ref[:, mine]], axis=0)
    collapse = lambda v: dot_nn(v, hot_back[mine, :])
    part = project(columns, sky, pb_ref[:, mine], collapse, row_mask(rows // 2, slots // 2)).astype(BF)
    for g in range(rows):
        send_ref[g] = part


def second_kernel(
    samples, got_ref, pack_ref, pb_ref, hot_ref, pb_back, hot_back, rhs_ref, map_ref, more_ref, send_ref, state_ref
):
    rhs = rhs_ref[...]
    more = more_ref[...]
    image = more * rhs - total_of(got_ref) * (1.0 / samples)
    rows = rhs.shape[0]
    columns, inv = columns_of(pack_ref)
    row_hot = row_mask(rows, columns.shape[1])
    image_map = bin_amps(image, columns, pb_back[...], hot_ref[...], row_hot)
    rr = total(rhs * rhs)
    alpha = rr / total(rhs * image)
    error = rhs - alpha * image
    new = total(error * error)
    beta = new / rr
    heading = error + beta * rhs
    binned = (1.0 + beta) * map_ref[...] - alpha * image_map
    sky = binned * inv
    part = project(columns, sky, pb_ref[...], lambda v: dot_nn(v, hot_back[...]), row_hot)
    quad = jnp.broadcast_to(total(binned * sky), (1, LANES))
    for g in range(rows):
        send_ref[g, 0:1, 0:LANES] = part[g : g + 1]
        send_ref[g, 0:1, LANES:] = quad
    scaled = more * heading
    state_ref[0] = alpha * rhs
    state_ref[1] = error
    state_ref[2] = heading
    state_ref[3] = scaled
    state_ref[4] = jnp.broadcast_to(new, (rows, LANES))
    state_ref[5] = jnp.broadcast_to(total(scaled * heading), (rows, LANES))


def last_kernel(samples, n_det, got_ref, state_ref, levels_ref, error_ref):
    me = lax.axis_index("pix") * n_det + lax.axis_index("det")
    acc = got_ref[0]
    for g in range(1, got_ref.shape[0]):
        acc = acc + got_ref[g]
    acc = acc * (1.0 / samples)
    mine = [state_ref[k, pl.ds(me, 1), :] for k in range(6)]
    levels, error, heading, scaled, new, curve = mine
    image = scaled - acc[:, 0:LANES]
    alpha = new / (curve - acc[:, LANES:])
    levels_ref[...] = levels + alpha * heading
    error_ref[...] = error - alpha * image


def call(kernel, outs, *args, scratch=()):
    vmem = pl.BlockSpec(memory_space=pltpu.VMEM)
    return pl.pallas_call(
        kernel,
        out_shape=outs,
        in_specs=[vmem] * len(args),
        out_specs=[vmem] * len(outs),
        scratch_shapes=scratch,
        compiler_params=pltpu.CompilerParams(vmem_limit_bytes=VMEM_LIMIT),
        cost_estimate=pl.CostEstimate(flops=10**8, bytes_accessed=4 * 10**6, transcendentals=0),
    )(*args)


def exchange(x):
    return lax.all_to_all(x, ("pix", "det"), split_axis=0, concat_axis=0, tiled=True)


def other_core(x):
    return lax.ppermute(x, "det", [(i, i ^ 1) for i in range(lax.axis_size("det"))])


def body(timestream, weights, block_owner, block_local, baseline_of):
    n_det, n_pix = lax.axis_size("det"), lax.axis_size("pix")
    rows = n_det * n_pix
    _, blocks, samples, pixels = weights.shape
    pch = pixels // n_det
    half = pch // 2
    slots = rows * CAP
    group = 32
    shape = jax.ShapeDtypeStruct
    hbm = functools.partial(pltpu.with_memory_space_constraint, memory_space=pltpu.HBM)
    owners = block_owner.reshape(1, blocks)
    give, *filling = pl.pallas_call(
        functools.partial(bin_kernel, n_det, n_pix, group),
        out_shape=[
            shape((rows, half, LANES), BF),
            *[shape((pixels, blocks), F32)] * 2,
            shape((blocks, pixels), F32),
            shape((blocks, n_pix * PB_DEV), BF),
        ],
        in_specs=[pl.BlockSpec(memory_space=pltpu.HBM)] * 4,
        out_specs=[pl.BlockSpec(memory_space=pltpu.VMEM)] * 5,
        scratch_shapes=[
            pltpu.VMEM((blocks // 2, 2 * samples, pixels), BF),
            pltpu.VMEM((blocks, samples), F32),
            *[pltpu.VMEM((1, blocks), jnp.int32)] * 2,
            *[pltpu.VMEM((blocks, pixels), F32)] * 2,
            pltpu.SemaphoreType.DMA((blocks // group + 1,)),
            pltpu.SemaphoreType.DMA((blocks // group + 3,)),
        ],
        compiler_params=pltpu.CompilerParams(vmem_limit_bytes=VMEM_LIMIT),
        cost_estimate=pl.CostEstimate(flops=10**8, bytes_accessed=2**25, transcendentals=0),
    )(hbm(timestream), weights.reshape(blocks // 2, 2 * samples, pixels), hbm(owners), hbm(block_local))
    took = other_core(give)
    mine, rest = call(
        functools.partial(fill_kernel, n_det, n_pix),
        [shape((rows, half, LANES), F32), shape((rows, half + 8, LANES), BF)],
        timestream, owners, block_local, baseline_of, *filling,
    )
    got = exchange(call(join_kernel, [shape((rows, pch + 8, LANES), BF)], mine, took, rest)[0])
    vector = shape((rows, NBASE_DEV), F32)
    part = shape((rows // 2, NBASE_DEV), F32)

    everyone = shape((rows, rows // 2, NBASE_DEV), BF)
    keep, give, col_t, inv, pb_hot, base_hot = call(
        functools.partial(owner_kernel, pch),
        [
            part, part, shape((pch, slots), BF), shape((pch, PB_DEV), F32),
            shape((PB_DEV, slots), BF), shape((NBASE_DEV, slots), BF),
        ],
        got,
        scratch=[pltpu.VMEM((rows, NBASE_DEV), F32), pltpu.VMEM((8, slots), F32)],
    )
    turned = call(
        turn_kernel,
        [shape((pch, slots + LANES), BF), shape((slots, PB_DEV), BF), shape((slots, NBASE_DEV), BF), vector],
        got, col_t, inv, pb_hot, base_hot,
    )
    took, pack, *backs, more = lax.optimization_barrier((other_core(give), *turned))
    other = other_core(pack)
    sent = call(sum_kernel, [everyone], keep, took)[0]
    sent, rhs, rhs_map = call(
        functools.partial(first_kernel, samples), [everyone, vector, shape((pch, PB_DEV), F32)], exchange(sent), pack, other, pb_hot, base_hot, *backs
    )
    sent, state = call(
        functools.partial(second_kernel, samples),
        [shape((rows, 1, 2 * LANES), F32), shape((6, rows, NBASE_DEV), F32)],
        exchange(sent), pack, pb_hot, base_hot, *backs, rhs, rhs_map, more,
    )
    own = shape((1, NBASE_DEV), F32)
    return tuple(call(functools.partial(last_kernel, samples, n_det), [own, own], exchange(sent), state))


def solution(mesh):
    placed = (
        P(AXES, None, None),
        P(AXES, None, None, None),
        P(AXES, None, None),
        P(AXES, None),
        P(AXES, None),
    )
    return jax.shard_map(
        body,
        mesh=mesh,
        in_specs=placed,
        out_specs=(P(AXES, None), P(AXES, None)),
        check_vma=False,
    )
```

```python
import functools

import jax
import jax.numpy as jnp
from jax import lax
from jax.experimental import pallas as pl
from jax.experimental.pallas import tpu as pltpu
from jax.sharding import PartitionSpec as P

PB_DEV = 64
NBASE_DEV = 128
CAP = 64
LANES = 128
AXES = ("det", "pix")
BF = jnp.bfloat16
F32 = jnp.float32
VMEM_LIMIT = 48 * 1024 * 1024


def dot_nn(a, b):
    return lax.dot_general(a, b, (((1,), (0,)), ((), ())), preferred_element_type=F32)


def dot_nt(a, b):
    return lax.dot_general(a, b, (((1,), (1,)), ((), ())), preferred_element_type=F32)


def split3(v):
    a = v.astype(BF)
    left = v - a.astype(F32)
    b = left.astype(BF)
    c = (left - b.astype(F32)).astype(BF)
    return a, b, c


def iota(shape, dim):
    return lax.broadcasted_iota(jnp.int32, shape, dim)


def column(row):
    n = row.shape[1]
    eye = (iota((n, n), 0) == iota((n, n), 1)).astype(F32).astype(BF)
    return dot_nt(eye, jnp.broadcast_to(row.astype(F32).astype(BF), (8, n)))[:, 0:1].astype(jnp.int32)


def hot(target, wide):
    return (iota((target.shape[0], wide), 1) == target).astype(F32).astype(BF)


def bin_kernel(
    n_det, n_pix, group, ts_hbm, w_hbm, own_hbm, loc_hbm,
    give_ref, hit_ref, dat_ref, col_ref, pb_hot,
    w_s, ts_s, own_s, loc_s, hit_s, dat_s, sem, small,
):
    blocks, samples, pixels = ts_s.shape[0], ts_s.shape[1], w_s.shape[2]
    steps = blocks // group - 1
    short = group // 2

    def copies(first, many, k):
        where, pairs = pl.ds(2 * first, 2 * many), pl.ds(first, many)
        return (
            pltpu.make_async_copy(ts_hbm.at[0, where], ts_s.at[where], small.at[k]),
            pltpu.make_async_copy(w_hbm.at[pairs], w_s.at[pairs], sem.at[k]),
        )

    def full(c):
        return copies(c * short, short, c)

    ends = [copies(steps * short + k * short // 2, short // 2, steps + k) for k in (0, 1)]

    indices = [
        pltpu.make_async_copy(src, dst, small.at[steps + 2 + k]) for k, (src, dst) in enumerate(((own_hbm, own_s), (loc_hbm, loc_s)))
    ]
    for copy in indices:
        copy.start()
    for piece in [full(c) for c in range(steps)] + ends:
        for copy in piece:
            copy.start()
    place = iota((samples, LANES), 1)
    ones = jnp.ones((pixels, LANES), BF)
    row = iota((8, 2 * samples), 0) - jnp.where(iota((8, 2 * samples), 1) < samples, 0, 3)

    def row_sums(first, many):
        acc = jnp.zeros((samples, LANES), F32)
        for j in range(2 * many):
            w = w_s[first + j // 2, (j % 2) * samples : (j % 2 + 1) * samples, :]
            if j % 3 == 2:
                sums = dot_nn(w, ones)
            else:
                w = w.astype(F32)
                halves = w[:, 0:LANES]
                for k in range(LANES, pixels, LANES):
                    halves = halves + w[:, k : k + LANES]
                sums = jnp.sum(halves, axis=1, keepdims=True)
            acc = jnp.where(place == j, sums, acc)
        return acc.T[0 : 2 * many]

    def beside(one, two):
        return jnp.concatenate([jnp.broadcast_to(v, (8, samples)) for v in (one, two)], axis=1)

    def terms(first, many, sums):
        for j in range(many):
            r = beside(sums[2 * j : 2 * j + 1], sums[2 * j + 1 : 2 * j + 2])
            at = 2 * (first + j)
            u = beside(ts_s[pl.ds(at, 1), :], ts_s[pl.ds(at + 1, 1), :])
            lhs = jnp.where(row == 0, r, jnp.where(row == 1, u, jnp.where(row == 2, 1.0, 0.0))).astype(BF)
            t = dot_nn(lhs, w_s[first + j])
            for k in (0, 1):
                where = pl.ds(at + k, 1)
                hit_s[where, :] = t[3 * k : 3 * k + 1]
                dat_s[where, :] = t[3 * k + 1 : 3 * k + 2]
                col_ref[where, :] = t[3 * k + 2 : 3 * k + 3]

    def wait(piece):
        for copy in piece:
            copy.wait()

    def step(c, sums):
        wait(full(c))
        after = row_sums(c * short, short)
        terms((c - 1) * short, short, sums)
        return after

    wait(full(0))
    sums = lax.fori_loop(1, steps, step, row_sums(0, short))
    begin, quarter = steps * short, short // 2
    wait(ends[0])
    after = row_sums(begin, quarter)
    terms(begin - short, short, sums)
    wait(ends[1])
    last = row_sums(begin + quarter, quarter)
    terms(begin, quarter, after)
    for copy in indices:
        copy.wait()
    pb_hot[...] = hot(column(own_s[...]) * PB_DEV + column(loc_s[...]), n_pix * PB_DEV)
    terms(begin + quarter, quarter, last)
    hit_ref[...] = hit_s[...].T
    dat_ref[...] = dat_s[...].T
    core = lax.rem(lax.axis_index("det"), 2)
    binned(n_det, n_pix, 1 - core, hit_ref, dat_ref, pb_hot, give_ref)


def pair(first, second, swap):
    low = iota(first.shape, 1) < CAP
    return jnp.where(low, first, swap(second)), jnp.where(low, swap(first), second)


def swap_halves(v):
    return pltpu.roll(v, CAP, 1)


def two_up(n_det, n_pix, first, second, ref):
    half = first.shape[0] // n_det
    for i in range(n_pix // 2):
        cols = slice(i * LANES, (i + 1) * LANES)
        for o, tile in zip((2 * i, 2 * i + 1), pair(first[:, cols], second[:, cols], swap_halves)):
            tile = tile.astype(ref.dtype)
            for d in range(n_det):
                ref[d * n_pix + o, 0:half, :] = tile[d * half : (d + 1) * half]


def binned(n_det, n_pix, which, hit_ref, dat_ref, pb_hot, ref):
    half = hit_ref.shape[0] // n_det // 2
    rows = [
        of[pl.ds(pl.multiple_of((2 * d + which) * half, half), half), :].astype(BF) for of in (hit_ref, dat_ref) for d in range(n_det)
    ]
    both = dot_nn(jnp.concatenate(rows, axis=0), pb_hot[...])
    two_up(n_det, n_pix, both[: n_det * half], both[n_det * half :], ref)


def fill_kernel(n_det, n_pix, ts_ref, own_ref, loc_ref, base_ref, hit_ref, dat_ref, col_ref, pb_hot, mine_ref, rest_ref):
    _, blocks, samples = ts_ref.shape
    own = column(own_ref[...])
    tri = (iota((blocks, blocks), 1) < iota((blocks, blocks), 0)).astype(F32).astype(BF)
    own_hot = (own == iota((blocks, LANES), 1)).astype(F32)
    before = dot_nn(tri, own_hot.astype(BF))
    slot = own * CAP + jnp.sum(before * own_hot, axis=1, keepdims=True).astype(jnp.int32)
    slot_hot = hot(slot, n_pix * CAP)
    core = lax.rem(lax.axis_index("det"), 2)
    binned(n_det, n_pix, core, hit_ref, dat_ref, pb_hot, mine_ref)
    col_t = col_ref[...].T.astype(BF)
    pch = col_t.shape[0] // n_det
    half = pch // 2
    rows = [col_t[(2 * d + k) * half : (2 * d + k + 1) * half] for k in (0, 1) for d in range(n_det)]
    both = dot_nn(jnp.concatenate(rows, axis=0), slot_hot)
    two_up(n_det, n_pix, both[: n_det * half], both[n_det * half :], rest_ref)

    sums = jnp.sum(ts_ref[0].T, axis=0, keepdims=True)
    w0, w1, w2 = [w.astype(F32) for w in split3(sums / jnp.sum(col_t.astype(F32), axis=0, keepdims=True))]
    r16 = iota((16, blocks), 0)
    lhs = jnp.where(r16 == 0, loc_ref[...].astype(F32), jnp.where(r16 == 8, base_ref[...].astype(F32), 0.0))
    lhs = jnp.where(r16 == 1, w0, jnp.where(r16 == 9, w1, jnp.where(r16 == 2, w2, lhs)))
    where = dot_nn(lhs.astype(BF), slot_hot)
    base_hot = (column(base_ref[...]) == iota((blocks, NBASE_DEV), 1)).astype(F32)
    count = jnp.sum(base_hot, axis=0, keepdims=True)
    r8 = iota((8, LANES), 0)
    for i in range(n_pix // 2):
        cols = slice(i * LANES, (i + 1) * LANES)
        for o, tile in zip((2 * i, 2 * i + 1), pair(where[0:8, cols], where[8:16, cols], swap_halves)):
            tile = jnp.where(r8 == 3, count, tile).astype(BF)
            for d in range(n_det):
                rest_ref[d * n_pix + o, half:, :] = tile


def join_kernel(mine_ref, took_ref, rest_ref, send_ref):
    rows, half, _ = mine_ref.shape
    for g in range(rows):
        send_ref[g, 0:half, :] = rest_ref[g, 0:half, :]
        send_ref[g, half : 2 * half, :] = (mine_ref[g] + took_ref[g].astype(F32)).astype(BF)
        send_ref[g, 2 * half :, :] = rest_ref[g, half:, :]


def split2(v):
    a = v.astype(BF)
    return a, (v - a.astype(F32)).astype(BF)


def total(v):
    return jnp.sum(jnp.sum(v, axis=0, keepdims=True), axis=1, keepdims=True)


def project(col_t, sky_t, pb_hot, collapse, row_hot, shift=None):
    rows = row_hot.shape[0]
    spread = dot_nn(sky_t.astype(BF), pb_hot)
    spread = spread if shift is None else spread - shift
    per_slot = jnp.sum(col_t.astype(F32) * spread, axis=0, keepdims=True)
    parts = [jnp.where(row_hot, p.astype(F32), 0.0).astype(BF) for p in split2(per_slot)]
    both = collapse(jnp.concatenate(parts, axis=0))
    return both[0:rows] + both[rows:]


def bin_amps(amps, col_t, pb_back, base_hot, row_hot):
    rows = row_hot.shape[0]
    both = dot_nn(jnp.concatenate(split2(amps), axis=0), base_hot)
    per_slot = jnp.sum(jnp.where(row_hot, both[0:rows] + both[rows:], 0.0), axis=0, keepdims=True)
    return dot_nn((col_t.astype(F32) * per_slot).astype(BF), pb_back)


def row_mask(rows, slots):
    return iota((rows, slots), 1) // CAP == iota((rows, slots), 0)


def halves_out(part, keep_ref, give_ref, work):
    work[...] = part
    half = keep_ref.shape[0]
    core = lax.rem(lax.axis_index("det"), 2)
    keep_ref[...] = work[pl.ds(pl.multiple_of(core * half, half), half), :]
    give_ref[...] = work[pl.ds(pl.multiple_of((1 - core) * half, half), half), :]


def sum_kernel(keep_ref, took_ref, send_ref):
    part = (keep_ref[...] + took_ref[...]).astype(BF)
    for g in range(send_ref.shape[0]):
        send_ref[g] = part


def total_of(got_ref, n_pix):
    sums = [None, None]
    for g in range(got_ref.shape[0]):
        core = (g // n_pix) % 2
        term = got_ref[g].astype(F32)
        sums[core] = term if sums[core] is None else sums[core] + term
    return jnp.concatenate(sums, axis=0)


def columns_of(pack_ref):
    slots = pack_ref.shape[1] - LANES
    inv = pack_ref[:, slots:].astype(F32)
    return pack_ref[:, :slots], inv[:, 0:PB_DEV] + inv[:, PB_DEV:]


def owner_kernel(pch, n_pix, got_ref, keep_ref, give_ref, pack_ref, pb_ref, hot_ref, more_ref, work, mean):
    rows = got_ref.shape[0]
    half = pch // 2
    slots = rows * CAP
    pb_of = iota((PB_DEV, LANES), 0).astype(F32).astype(BF)
    base_of = iota((NBASE_DEV, LANES), 0).astype(F32).astype(BF)
    yes, no = jnp.ones((1, LANES), BF), jnp.zeros((1, LANES), BF)
    maps = [jnp.zeros((half, LANES), F32), jnp.zeros((half, LANES), F32)]
    for g in range(rows):
        core = (g // n_pix) % 2
        maps[core] = maps[core] + got_ref[g, half : 2 * half, :].astype(F32)
    for i in range(rows // 2):
        cols = slice(i * LANES, (i + 1) * LANES)
        halves = pair(got_ref[2 * i, 0:half, :].astype(F32), got_ref[2 * i + 1, 0:half, :].astype(F32), swap_halves)
        pack_ref[0:half, cols] = halves[0].astype(BF)
        pack_ref[half:, cols] = halves[1].astype(BF)
        tiles = [got_ref[2 * i + k, 2 * half :, :].astype(F32) for k in (0, 1)]
        one, two = pair(*tiles, swap_halves)
        pb_ref[:, cols] = jnp.where(pb_of == one[0:1].astype(BF), yes, no)
        hot_ref[:, cols] = jnp.where(base_of == two[0:1].astype(BF), yes, no)
        mean[0:1, cols] = one[1:2] + two[1:2] + one[2:3]
        for k in (0, 1):
            more_ref[2 * i + k : 2 * i + k + 1, :] = tiles[k][3:4] + 1.0
    maps = jnp.concatenate(maps, axis=0)
    inv = 1.0 / (maps[:, 0:PB_DEV] + 1.0)
    pack_ref[:, slots:] = jnp.concatenate([v.astype(F32) for v in split2(inv)], axis=1).astype(BF)
    sky = maps[:, PB_DEV:] * inv
    collapse = lambda v: dot_nt(v, hot_ref[...])
    part = project(pack_ref[:, :slots], sky, pb_ref[...], collapse, row_mask(rows, slots), mean[0:1, :])
    halves_out(part, keep_ref, give_ref, work)


def turn_kernel(pb_ref, hot_ref, pb_back_ref, hot_back_ref):
    for k in range(0, pb_ref.shape[1], LANES):
        for ref, back in ((pb_ref, pb_back_ref), (hot_ref, hot_back_ref)):
            back[k : k + LANES, :] = ref[:, k : k + LANES].astype(F32).T.astype(BF)


def first_kernel(samples, n_pix, got_ref, pack_ref, other_ref, pb_ref, hot_ref, pb_back, hot_back, send_ref, rhs_ref, map_ref):
    rhs = total_of(got_ref, n_pix) * (-1.0 / samples)
    rhs_ref[...] = rhs
    rows = rhs.shape[0]
    slots = rows * CAP
    columns, inv = zip(columns_of(pack_ref), columns_of(other_ref))
    binned = bin_amps(rhs, jnp.concatenate(columns, axis=0), pb_back[...], hot_ref[...], row_mask(rows, slots))
    map_ref[...] = binned[: pack_ref.shape[0]]
    sky = binned * jnp.concatenate(inv, axis=0)
    core = lax.rem(lax.axis_index("det"), 2)
    mine = pl.ds(pl.multiple_of(core * (slots // 2), slots // 2), slots // 2)
    columns = jnp.concatenate([pack_ref[:, mine], other_ref[:, mine]], axis=0)
    collapse = lambda v: dot_nn(v, hot_back[mine, :])
    part = project(columns, sky, pb_ref[:, mine], collapse, row_mask(rows // 2, slots // 2)).astype(BF)
    for g in range(rows):
        send_ref[g] = part


def second_kernel(
    samples, n_pix, got_ref, pack_ref, pb_ref, hot_ref, pb_back, hot_back, rhs_ref, map_ref, more_ref, send_ref, state_ref
):
    rhs = rhs_ref[...]
    more = more_ref[...]
    image = more * rhs - total_of(got_ref, n_pix) * (1.0 / samples)
    rows = rhs.shape[0]
    columns, inv = columns_of(pack_ref)
    row_hot = row_mask(rows, columns.shape[1])
    image_map = bin_amps(image, columns, pb_back[...], hot_ref[...], row_hot)
    rr = total(rhs * rhs)
    alpha = rr / total(rhs * image)
    error = rhs - alpha * image
    new = total(error * error)
    beta = new / rr
    heading = error + beta * rhs
    binned = (1.0 + beta) * map_ref[...] - alpha * image_map
    sky = binned * inv
    part = project(columns, sky, pb_ref[...], lambda v: dot_nn(v, hot_back[...]), row_hot)
    quad = jnp.broadcast_to(total(binned * sky), (1, LANES))
    for g in range(rows):
        send_ref[g, 0:1, 0:LANES] = part[g : g + 1]
        send_ref[g, 0:1, LANES:] = quad
    scaled = more * heading
    state_ref[0] = alpha * rhs
    state_ref[1] = error
    state_ref[2] = heading
    state_ref[3] = scaled
    state_ref[4] = jnp.broadcast_to(new, (rows, LANES))
    state_ref[5] = jnp.broadcast_to(total(scaled * heading), (rows, LANES))


def last_kernel(samples, n_pix, got_ref, state_ref, levels_ref, error_ref):
    me = lax.axis_index("det") * n_pix + lax.axis_index("pix")
    acc = got_ref[0]
    for g in range(1, got_ref.shape[0]):
        acc = acc + got_ref[g]
    acc = acc * (1.0 / samples)
    mine = [state_ref[k, pl.ds(me, 1), :] for k in range(6)]
    levels, error, heading, scaled, new, curve = mine
    image = scaled - acc[:, 0:LANES]
    alpha = new / (curve - acc[:, LANES:])
    levels_ref[...] = levels + alpha * heading
    error_ref[...] = error - alpha * image


def call(kernel, outs, *args, scratch=()):
    vmem = pl.BlockSpec(memory_space=pltpu.VMEM)
    return pl.pallas_call(
        kernel,
        out_shape=outs,
        in_specs=[vmem] * len(args),
        out_specs=[vmem] * len(outs),
        scratch_shapes=scratch,
        compiler_params=pltpu.CompilerParams(vmem_limit_bytes=VMEM_LIMIT),
        cost_estimate=pl.CostEstimate(flops=10**8, bytes_accessed=4 * 10**6, transcendentals=0),
    )(*args)


def exchange(x):
    return lax.all_to_all(x, AXES, split_axis=0, concat_axis=0, tiled=True)


def other_core(x):
    return lax.ppermute(x, "det", [(i, i ^ 1) for i in range(lax.axis_size("det"))])


def body(timestream, weights, block_owner, block_local, baseline_of):
    n_det, n_pix = lax.axis_size("det"), lax.axis_size("pix")
    rows = n_det * n_pix
    _, blocks, samples, pixels = weights.shape
    pch = pixels // n_det
    half = pch // 2
    slots = rows * CAP
    group = 32
    shape = jax.ShapeDtypeStruct
    hbm = functools.partial(pltpu.with_memory_space_constraint, memory_space=pltpu.HBM)
    owners = block_owner.reshape(1, blocks)
    give, *filling = pl.pallas_call(
        functools.partial(bin_kernel, n_det, n_pix, group),
        out_shape=[
            shape((rows, half, LANES), BF),
            *[shape((pixels, blocks), F32)] * 2,
            shape((blocks, pixels), F32),
            shape((blocks, n_pix * PB_DEV), BF),
        ],
        in_specs=[pl.BlockSpec(memory_space=pltpu.HBM)] * 4,
        out_specs=[pl.BlockSpec(memory_space=pltpu.VMEM)] * 5,
        scratch_shapes=[
            pltpu.VMEM((blocks // 2, 2 * samples, pixels), BF),
            pltpu.VMEM((blocks, samples), F32),
            *[pltpu.VMEM((1, blocks), jnp.int32)] * 2,
            *[pltpu.VMEM((blocks, pixels), F32)] * 2,
            pltpu.SemaphoreType.DMA((blocks // group + 1,)),
            pltpu.SemaphoreType.DMA((blocks // group + 3,)),
        ],
        compiler_params=pltpu.CompilerParams(vmem_limit_bytes=VMEM_LIMIT),
        cost_estimate=pl.CostEstimate(flops=10**8, bytes_accessed=2**25, transcendentals=0),
    )(hbm(timestream), weights.reshape(blocks // 2, 2 * samples, pixels), hbm(owners), hbm(block_local))
    took = other_core(give)
    mine, rest = call(
        functools.partial(fill_kernel, n_det, n_pix),
        [shape((rows, half, LANES), F32), shape((rows, half + 8, LANES), BF)],
        timestream, owners, block_local, baseline_of, *filling,
    )
    got = exchange(call(join_kernel, [shape((rows, pch + 8, LANES), BF)], mine, took, rest)[0])
    vector = shape((rows, NBASE_DEV), F32)
    part = shape((rows // 2, NBASE_DEV), F32)

    everyone = shape((rows, rows // 2, NBASE_DEV), BF)
    keep, give, pack, pb_hot, base_hot, more = call(
        functools.partial(owner_kernel, pch, n_pix),
        [part, part, shape((pch, slots + LANES), BF), shape((PB_DEV, slots), BF), shape((NBASE_DEV, slots), BF), vector],
        got,
        scratch=[pltpu.VMEM((rows, NBASE_DEV), F32), pltpu.VMEM((8, slots), F32)],
    )
    backs = call(turn_kernel, [shape((slots, PB_DEV), BF), shape((slots, NBASE_DEV), BF)], pb_hot, base_hot)
    took, pack, *backs = lax.optimization_barrier((other_core(give), pack, *backs))
    other = other_core(pack)
    sent = call(sum_kernel, [everyone], keep, took)[0]
    sent, rhs, rhs_map = call(
        functools.partial(first_kernel, samples, n_pix), [everyone, vector, shape((pch, PB_DEV), F32)], exchange(sent), pack, other, pb_hot, base_hot, *backs
    )
    sent, state = call(
        functools.partial(second_kernel, samples, n_pix),
        [shape((rows, 1, 2 * LANES), F32), shape((6, rows, NBASE_DEV), F32)],
        exchange(sent), pack, pb_hot, base_hot, *backs, rhs, rhs_map, more,
    )
    own = shape((1, NBASE_DEV), F32)
    return tuple(call(functools.partial(last_kernel, samples, n_pix), [own, own], exchange(sent), state))


def solution(mesh):
    placed = (
        P(AXES, None, None),
        P(AXES, None, None, None),
        P(AXES, None, None),
        P(AXES, None),
        P(AXES, None),
    )
    return jax.shard_map(
        body,
        mesh=mesh,
        in_specs=placed,
        out_specs=(P(AXES, None), P(AXES, None)),
        check_vma=False,
    )
```
